256 devices in a mesh: group: 8 (over x, core), brick: 32 (over y, z).
Axes of the slice: x: 4, y: 4, z: 8, core: 2. Of those that a mesh axis runs over, the one named last changes fastest.
Arguments:
- noise_level0: float32 [8, 64, 16], P('group', 'brick'), may hold values from -6 to 6
- noise_level1: float32 [16, 128, 32], P('group', 'brick'), may hold values from -6 to 6
- noise_level2: float32 [32, 256, 64], P('group', 'brick'), may hold values from -6 to 6
- noise_level3: float32 [64, 512, 128], P('group', 'brick'), may hold values from -6 to 6
- noise_level4: float32 [128, 1024, 256], P('group', 'brick'), may hold values from -6 to 6
- refine_kernels: float32 [4, 8, 27], replicated, may hold values from -1.25 to 1.25
- noise_kernels: float32 [4, 8, 8], replicated, may hold values from -2 to 2
- cotangent: float32 [128, 1024, 256], P('group', 'brick'), may hold values from -6 to 6
Outputs:
- density: float32 [128, 1024, 256], P('group', 'brick')
- grad_level0: float32 [8, 64, 16], P('group', 'brick')
- grad_level1: float32 [16, 128, 32], P('group', 'brick')
- grad_level2: float32 [32, 256, 64], P('group', 'brick')
- grad_level3: float32 [64, 512, 128], P('group', 'brick')
- grad_level4: float32 [128, 1024, 256], P('group', 'brick')
The draws below stay inside these ranges and needn't reach their ends.
All inputs are finite; a program needn't handle non-finite values.
Results may differ from the reference program's by a relative error of at most 0.0002.
Values sent between devices are 32-bit elements; how exact they have to be, the bound alone decides.
A program may use at most 128 MiB of HBM per device.

```python
import jax
import jax.numpy as jnp
from jax import lax

Z0 = 16
LEVELS = 4
NX0 = 8
NY0 = 64


def levels(stream_key, dims, shards, low, high):
    loudness = 1.0
    for axis_at, shards_of in shards:
        draws = jax.random.uniform(jax.random.fold_in(jax.random.fold_in(stream_key, 6), axis_at), (shards_of,), jnp.float32, low / len(shards), high / len(shards))
        loudness = loudness * jnp.repeat(jnp.exp(draws), dims[axis_at] // shards_of).reshape((-1,) + (1,) * (len(dims) - 1 - axis_at))
    return loudness


def normal_values(stream_key, extent, scale, reach, pieces=(), dtype=jnp.bfloat16):
    loudness = levels(stream_key, extent, pieces, -0.22, 0.18) if pieces else 1.0
    array = jax.random.normal(stream_key, extent, jnp.float32) * scale * loudness
    return jnp.minimum(jnp.maximum(array, -reach), reach).astype(dtype)


def setup_inputs(seed: int = 0) -> dict:
    key_of = jax.random.split(jax.random.key(seed), 9)
    return {
        "noise_level0": normal_values(key_of[0], (NX0, NY0, Z0), 1.0, 6.0, ((0, 8), (1, 32)), jnp.float32),
        "noise_level1": normal_values(key_of[1], (NX0 * 2, NY0 * 2, Z0 * 2), 1.0, 6.0, ((0, 8), (1, 32)), jnp.float32),
        "noise_level2": normal_values(key_of[2], (NX0 * 4, NY0 * 4, Z0 * 4), 1.0, 6.0, ((0, 8), (1, 32)), jnp.float32),
        "noise_level3": normal_values(key_of[3], (NX0 * 8, NY0 * 8, Z0 * 8), 1.0, 6.0, ((0, 8), (1, 32)), jnp.float32),
        "noise_level4": normal_values(key_of[4], (NX0 * 16, NY0 * 16, Z0 * 16), 1.0, 6.0, ((0, 8), (1, 32)), jnp.float32),
        "refine_kernels": normal_values(key_of[5], (LEVELS, 8, 27), 27 ** -0.5, 1.25, (), jnp.float32),
        "noise_kernels": normal_values(key_of[6], (LEVELS, 8, 8), 8 ** -0.5, 2.0, (), jnp.float32),
        "cotangent": normal_values(key_of[7], (NX0 * 16, NY0 * 16, Z0 * 16), 1.0, 6.0, ((0, 8), (1, 32)), jnp.float32),
    }


def to_blocks(values):
    size_x, size_y, size_z = values.shape
    rows_x, rows_y, rows_z = (size_x // 2, size_y // 2, size_z // 2)
    shaped = values.reshape(rows_x, 2, rows_y, 2, rows_z, 2)
    return shaped.transpose(1, 3, 5, 0, 2, 4).reshape(8, rows_x, rows_y, rows_z)

def from_blocks(blocks):
    rows_x, rows_y, rows_z = (blocks.shape[1], blocks.shape[2], blocks.shape[3])
    shaped = blocks.reshape(2, 2, 2, rows_x, rows_y, rows_z)
    return shaped.transpose(3, 0, 4, 1, 5, 2).reshape(2 * rows_x, 2 * rows_y, 2 * rows_z)

def expand(padded, kernel):
    rows_x, rows_y, rows_z = (padded.shape[0] - 2, padded.shape[1] - 2, padded.shape[2] - 2)
    total = jnp.zeros((8, rows_x, rows_y, rows_z), jnp.float32)
    for along_x in range(3):
        for along_y in range(3):
            for along_z in range(3):
                column = 9 * along_x + 3 * along_y + along_z
                window = padded[along_x:along_x + rows_x, along_y:along_y + rows_y, along_z:along_z + rows_z]
                total = total + kernel[:, column][:, None, None, None] * window[None]
    return total

def refine(coarse, kernel, covariance, noise):
    blocks = expand(jnp.pad(coarse, 1), kernel)
    blocks = blocks + jnp.einsum('uv,vabc->uabc', covariance, to_blocks(noise), precision=lax.Precision.HIGHEST)
    return from_blocks(blocks)

def reference(noise_level0, noise_level1, noise_level2, noise_level3, noise_level4, refine_kernels, noise_kernels, cotangent):

    def forward(noises):
        field = noises[0]
        for level in range(LEVELS):
            field = refine(field, refine_kernels[level], noise_kernels[level], noises[level + 1])
        return field
    noises = (noise_level0, noise_level1, noise_level2, noise_level3, noise_level4)
    density, pullback = jax.vjp(forward, noises)
    grads = pullback(cotangent)[0]
    return (density, grads[0], grads[1], grads[2], grads[3], grads[4])
```

```python
import jax
import jax.numpy as jnp
from jax import lax
from jax.experimental import pallas as pl
from jax.experimental.pallas import tpu as pltpu
from jax.sharding import PartitionSpec as P

LEVELS = 4
F32 = jnp.float32
BF16 = jnp.bfloat16
MESH = pl.DeviceIdType.MESH

NEAR = [(dx, dy) for dx in (-1, 0, 1) for dy in (-1, 0, 1) if (dx, dy) != (0, 0)]
FAR = [(dx, dy) for dx in (-2, 2) for dy in (-1, 0, 1)]
DIRS = NEAR + FAR


def up8(n):
    return -(-n // 8) * 8


class Plan:
    def __init__(self, shapes):
        self.block = shapes
        self.pairs = {}
        for level in range(1, LEVELS + 1):
            grow = 0 if level == LEVELS else 2
            self.pairs[level] = (shapes[level][0] // 2 + grow, shapes[level][1] // 2 + grow)
        self.rows = {level: up8(2 * ny) for level, (_, ny) in self.pairs.items()}
        self.ext = [
            (shapes[level][0] + 4, up8(shapes[level][1] + 4), 128) for level in range(LEVELS)
        ]
        self.pieces = {}
        self.offset = {}
        total = 0
        for dx, dy in DIRS:
            rows = 0
            pieces = []
            for level in range(LEVELS):
                if abs(dx) == 2 and level > 0:
                    continue
                bx, by = shapes[level][0], shapes[level][1]
                count_x = bx if dx == 0 else min(2, bx)
                count_y = by if dy == 0 else 2
                pieces.append((level, rows, count_x, count_y))
                rows += count_x * count_y
            self.pieces[dx, dy] = pieces
            self.offset[dx, dy] = (total, up8(rows))
            total += up8(rows)
        self.message_rows = total


def inner(step, size):
    if step == 0 or size == 1:
        return 2
    return 2 if step < 0 else size


def outer(step, size):
    if step == 0:
        return 2
    if size == 1:
        return 2 + step
    return 0 if step < 0 else size + 2


def lane_iota(shape):
    return lax.broadcasted_iota(jnp.int32, shape, len(shape) - 1)


def row_iota(shape):
    return lax.broadcasted_iota(jnp.int32, shape, len(shape) - 2)


def split(values):
    high = values.astype(BF16)
    return high, (values - high.astype(F32)).astype(BF16)


def select_dot(values, matrix):
    high, low = split(values)
    return jnp.dot(high, matrix, preferred_element_type=F32) + jnp.dot(
        low, matrix, preferred_element_type=F32
    )


def merge_matrix(size, width):
    row, col = row_iota((256, width)), lane_iota((256, width))
    parity = (row >= 128).astype(jnp.int32)
    at = row - 128 * parity
    return jnp.where((col == 2 * at + parity) & (at < size), 1.0, 0.0).astype(BF16)


def part_matrix(size, width):
    row, col = row_iota((width, 256)), lane_iota((width, 256))
    parity = (col >= 128).astype(jnp.int32)
    at = col - 128 * parity
    return jnp.where((row == 2 * at + parity) & (at < size), 1.0, 0.0).astype(BF16)


def parities():
    shape = (8, 128)
    return row_iota(shape) % 2 == 0, lane_iota(shape) % 2 == 0


def noise_patterns(read, store, transpose):
    even_row, even_lane = parities()
    for p in range(2):
        for other in range(2):
            for dq in range(2):
                for dr in range(2):
                    value = {}
                    for q in range(2):
                        for r in range(2):
                            here = 4 * p + 2 * q + r
                            there = 4 * other + 2 * (q ^ dq) + (r ^ dr)
                            value[q, r] = read(there, here) if transpose else read(here, there)
                    store(
                        p * 8 + other * 4 + dq * 2 + dr,
                        jnp.where(
                            even_row,
                            jnp.where(even_lane, value[0, 0], value[0, 1]),
                            jnp.where(even_lane, value[1, 0], value[1, 1]),
                        ),
                    )


def swaps(tile):
    even_row, even_lane = parities()

    def lanes(v):
        return jnp.where(even_lane, pltpu.roll(v, 127, 1), pltpu.roll(v, 1, 1))

    turned = jnp.where(even_row, pltpu.roll(tile, 7, 0), pltpu.roll(tile, 1, 0))
    return [tile, lanes(tile), turned, lanes(turned)]


def mix(first, second, weights):
    terms = swaps(first) + swaps(second)
    results = []
    for p in range(2):
        total = weights[p * 8] * terms[0]
        for at in range(1, 8):
            total = total + weights[p * 8 + at] * terms[at]
        results.append(total)
    return results


def shift_down(values, size):
    lane = lane_iota(values.shape)
    return jnp.where((lane > 0) & (lane < size), pltpu.roll(values, 1, 1), 0.0)


def shift_up(values, size):
    lane = lane_iota(values.shape)
    return jnp.where(lane < size - 1, pltpu.roll(values, 127, 1), 0.0)


def main_kernel(
    plan,
    noise0, noise1, noise2, noise3, refine_k, noise_k, cotangent,
    fine_out, grad0, grad1, grad2, grad3,
    ext0, ext1, ext2, ext3, part0, part1, part2, part3,
    field1, field2, field3, grads1, grads2, grads3,
    pattern, mixing, mixing_t, cot, shifted, spread, sums, split_g, taps, pooled,
    send_a, recv_a, send_b, recv_b,
    cot_sem, send_a_sem, recv_a_sem, send_b_sem, recv_b_sem,
):
    group, brick = lax.axis_index("group"), lax.axis_index("brick")
    groups, bricks = lax.axis_size("group"), lax.axis_size("brick")
    ext = [ext0, ext1, ext2, ext3]
    part = [part0, part1, part2, part3]
    field = [ext0, field1, field2, field3]
    grads = [part0, grads1, grads2, grads3]

    def neighbour(dx, dy):
        return (
            lax.rem(group + (dx + groups), groups),
            lax.rem(brick + (dy + bricks), bricks),
        )

    barrier = pltpu.get_barrier_semaphore()
    for dx, dy in DIRS:
        pl.semaphore_signal(barrier, inc=1, device_id=neighbour(dx, dy), device_id_type=MESH)

    cot_chunks = cot_sem.shape[0]
    chunk = cot.shape[0] // cot_chunks
    cot_copies = []
    for at in range(cot_chunks):
        copy = pltpu.make_async_copy(
            cotangent.at[pl.ds(at * chunk, chunk)], cot.at[pl.ds(at * chunk, chunk)], cot_sem.at[at]
        )
        copy.start()
        cot_copies.append(copy)

    for level, source in enumerate((noise0, noise1, noise2, noise3)):
        bx, by, size = plan.block[level]
        ext[level][...] = jnp.zeros(ext[level].shape, F32)
        if level:
            grads[level][...] = jnp.zeros(grads[level].shape, F32)
        part[level][...] = jnp.zeros(part[level].shape, F32)
        ext[level][2 : 2 + bx, 2 : 2 + by, 0:size] = source[...]

    def pack(source, target, start_of, sign):
        for dx, dy in DIRS:
            base, _ = plan.offset[dx, dy]
            for level, row, count_x, count_y in plan.pieces[dx, dy]:
                bx, by, _ = plan.block[level]
                x0, y0 = start_of(sign * dx, bx), start_of(sign * dy, by)
                for i in range(count_x):
                    target[pl.ds(base + row + i * count_y, count_y), :] = source[level][
                        x0 + i, y0 : y0 + count_y, :
                    ]

    def unpack(source, target, start_of, add):
        for dx, dy in DIRS:
            base, _ = plan.offset[dx, dy]
            for level, row, count_x, count_y in plan.pieces[dx, dy]:
                bx, by, _ = plan.block[level]
                x0, y0 = start_of(-dx, bx), start_of(-dy, by)
                for i in range(count_x):
                    value = source[pl.ds(base + row + i * count_y, count_y), :]
                    if add:
                        value = value + target[level][x0 + i, y0 : y0 + count_y, :]
                    target[level][x0 + i, y0 : y0 + count_y, :] = value

    def copies(source, target, send_sem, recv_sem):
        made = []
        for at, (dx, dy) in enumerate(DIRS):
            base, rows = plan.offset[dx, dy]
            made.append(
                pltpu.make_async_remote_copy(
                    src_ref=source.at[pl.ds(base, rows)],
                    dst_ref=target.at[pl.ds(base, rows)],
                    send_sem=send_sem.at[at],
                    recv_sem=recv_sem.at[at],
                    device_id=neighbour(dx, dy),
                    device_id_type=MESH,
                )
            )
        return made

    send_a[...] = jnp.zeros(send_a.shape, F32)
    send_b[...] = jnp.zeros(send_b.shape, F32)
    pack(ext, send_a, inner, 1)
    pl.semaphore_wait(barrier, len(DIRS))
    out_a = copies(send_a, recv_a, send_a_sem, recv_a_sem)
    for copy in out_a:
        copy.start()

    even_row, _ = parities()

    def build(level, carry):
        for o in range(27):
            for p in range(2):
                for r in range(2):
                    pattern[level, o * 4 + p * 2 + r] = jnp.where(
                        even_row,
                        refine_k[level, 4 * p + r, o],
                        refine_k[level, 4 * p + 2 + r, o],
                    )
        return carry

    lax.fori_loop(0, LEVELS, build, 0)

    def build_mixing(level, carry):
        def read(u, v):
            return noise_k[level, u, v]

        def store(at, value):
            mixing[level, at] = value

        def store_t(at, value):
            mixing_t[level, at] = value

        noise_patterns(read, store, False)
        noise_patterns(read, store_t, True)
        return carry

    lax.fori_loop(0, LEVELS - 1, build_mixing, 0)

    def inside(level, x_at, shape, first_row, first_x):
        bx, by, _ = plan.block[level]
        y = row_iota(shape) + (brick * by - 2 + first_row)
        x = group * bx - 2 + first_x + x_at
        limit = jnp.where((x >= 0) & (x < groups * bx), bricks * by, 0)
        return (y >= 0) & (y < limit)

    def tile_rows(at):
        return pl.ds(8 * at, 8)

    def adjoint(level):
        nx, ny = plan.pairs[level]
        rows = plan.rows[level]
        size = plan.block[level][2] // 2
        tiles = rows // 8
        if level == LEVELS:
            matrix = part_matrix(size, 256)
            for at in range(cot_chunks):
                cot_copies[at].wait()

            def part_chunk(at, carry):
                rows_in = cot[pl.ds(at * chunk, chunk)].reshape(chunk * rows, 256)
                both = select_dot(rows_in, matrix)
                for r in range(2):
                    split_g[r, pl.ds(at * chunk, chunk), 0:rows, :] = both[
                        :, 128 * r : 128 * (r + 1)
                    ].reshape(chunk, rows, 128)
                return carry

            lax.fori_loop(0, cot_chunks, part_chunk, 0)
        else:
            both = select_dot(
                grads[level][:, 0:rows, :].reshape(2 * nx * rows, 128), part_matrix(size, 128)
            )
            for r in range(2):
                split_g[r, 0 : 2 * nx, 0:rows, :] = both[:, 128 * r : 128 * (r + 1)].reshape(
                    2 * nx, rows, 128
                )

        for tap in range(9):
            for edge in (0, nx + 1):
                taps[tap, edge, 0:rows, :] = jnp.zeros((rows, 128), F32)

        for s in (1, 0, 2):
            weights = [pattern[level - 1, s * 36 + at] for at in range(36)]

            def step(i, carry):
                for tile in range(tiles):
                    here = tile_rows(tile)
                    values = [split_g[r, 2 * i + p, here, :] for p in range(2) for r in range(2)]
                    for tap in range(9):
                        total = weights[tap * 4] * values[0]
                        for at in range(1, 4):
                            total = total + weights[tap * 4 + at] * values[at]
                        if s != 1:
                            total = total + taps[tap, i + s, here, :]
                        taps[tap, i + s, here, :] = total
                return carry

            lax.fori_loop(0, nx, step, 0)

        target = grads[level - 1]
        first = 1 if level == LEVELS else 0

        def combine(x, carry):
            for t in range(3):
                pooled[t, 0:8, :] = jnp.zeros((8, 128), F32)
                pooled[t, pl.ds(8 + rows, 8), :] = jnp.zeros((8, 128), F32)
                for tile in range(tiles):
                    here = tile_rows(tile)
                    pooled[t, pl.ds(8 + 8 * tile, 8), :] = (
                        taps[3 * t + 1, x, here, :]
                        + shift_up(taps[3 * t, x, here, :], size)
                        + shift_down(taps[3 * t + 2, x, here, :], size)
                    )
            total = None
            for t in range(3):
                for q in range(2):
                    value = pooled[t, pl.ds(8 - 2 * t + q, ny + 2, stride=2), :]
                    total = value if total is None else total + value
            keep = inside(level - 1, x, (ny + 2, 128), first, first)
            target[x + first, first : first + ny + 2, :] = jnp.where(keep, total, 0.0)
            return carry

        lax.fori_loop(0, nx + 2, combine, 0)

    def mix_level(level, source, target, weights_of, masked):
        nx, _ = plan.pairs[level]
        weights = [weights_of[level - 1, at] for at in range(16)]

        def step(i, carry):
            for tile in range(plan.rows[level] // 8):
                here = tile_rows(tile)
                mixed = mix(source[2 * i, here, :], source[2 * i + 1, here, :], weights)
                for p in range(2):
                    value = mixed[p]
                    if masked:
                        value = value + target[2 * i + p, here, :]
                        keep = inside(level, 2 * i + p, (8, 128), 8 * tile, 0)
                        value = jnp.where(keep, value, 0.0)
                    target[2 * i + p, here, :] = value
            return carry

        lax.fori_loop(0, nx, step, 0)

    for level in range(LEVELS, 0, -1):
        adjoint(level)
        if level > 1:
            mix_level(level - 1, grads[level - 1], part[level - 1], mixing_t, False)

    pack(part, send_b, outer, 1)
    out_b = copies(send_b, recv_b, send_b_sem, recv_b_sem)
    for copy in out_b:
        copy.start()

    for copy in out_a:
        copy.wait_recv()
    unpack(recv_a, ext, outer, False)
    for x in range(ext0.shape[0]):
        keep = inside(0, x, ext0.shape[1:], 0, 0)
        ext0[x] = jnp.where(keep, ext0[x], 0.0)

    def forward(level):
        nx, ny = plan.pairs[level]
        rows = plan.rows[level]
        size = plan.block[level][2] // 2
        first = 1 if level == LEVELS else 0
        source = field[level - 1]
        count = up8(ny + 2)
        target = fine_out if level == LEVELS else sums

        def widen(x, carry):
            for tile in range(count // 8):
                value = source[x + first, pl.ds(first + 8 * tile, 8), :]
                for w, moved in enumerate((shift_down(value, size), value, shift_up(value, size))):
                    for q in range(2):
                        spread[w, x, pl.ds(16 * tile + q, 8, stride=2), :] = moved
            return carry

        lax.fori_loop(0, nx + 2, widen, 0)

        for s in range(3):
            weights = [pattern[level - 1, s * 36 + at] for at in range(36)]

            def step(i, carry):
                for tile in range(rows // 8):
                    here = tile_rows(tile)
                    totals = [None] * 4
                    for tap in range(9):
                        value = spread[tap % 3, i + s, pl.ds(8 * tile + 2 * (tap // 3), 8), :]
                        for at in range(4):
                            term = weights[tap * 4 + at] * value
                            totals[at] = term if totals[at] is None else totals[at] + term
                    for at in range(4):
                        p, r = at // 2, at % 2
                        value = totals[at]
                        if s:
                            value = value + target[r, 2 * i + p, here, :]
                        target[r, 2 * i + p, here, :] = value
                return carry

            lax.fori_loop(0, nx, step, 0)

        if level < LEVELS:
            both = jnp.concatenate(
                [sums[r, 0 : 2 * nx, 0:rows, :].reshape(2 * nx * rows, 128) for r in range(2)],
                axis=1,
            )
            fine = select_dot(both, merge_matrix(size, 128))
            field[level][:, 0:rows, :] = fine.reshape(2 * nx, rows, 128)
            mix_level(level, ext[level], field[level], mixing, True)

    for level in range(1, LEVELS + 1):
        forward(level)

    for copy in out_b:
        copy.wait_recv()
    unpack(recv_b, part, inner, True)
    for level, target in enumerate((grad0, grad1, grad2, grad3)):
        bx, by, size = plan.block[level]
        target[...] = part[level][2 : 2 + bx, 2 : 2 + by, 0:size]
    for copy in out_a + out_b:
        copy.wait_send()


def finish_kernel(
    fine, noise, cotangent, noise_k, in0, in1, in2, in3,
    density, grad, grad0, grad1, grad2, grad3, mixing, mixing_t,
):
    @pl.when(pl.program_id(0) == 0)
    def _():
        def read(u, v):
            return noise_k[LEVELS - 1, u, v]

        def store(at, value):
            mixing[at] = value

        def store_t(at, value):
            mixing_t[at] = value

        noise_patterns(read, store, False)
        noise_patterns(read, store_t, True)
        for source, target in ((in0, grad0), (in1, grad1), (in2, grad2), (in3, grad3)):
            target[...] = source[...]

    size_x, rows, _ = noise.shape
    both = jnp.concatenate([fine[r].reshape(size_x * rows, 128) for r in range(2)], axis=1)
    density[...] = select_dot(both, merge_matrix(128, 256)).reshape(size_x, rows, 256)
    for source, target, weights_of, add in (
        (noise, density, mixing, True),
        (cotangent, grad, mixing_t, False),
    ):
        weights = [weights_of[at] for at in range(16)]

        def step(i, carry):
            for tile in range(rows // 8):
                for half in range(2):
                    here, lanes = pl.ds(8 * tile, 8), pl.ds(128 * half, 128)
                    mixed = mix(
                        source[2 * i, here, lanes], source[2 * i + 1, here, lanes], weights
                    )
                    for p in range(2):
                        value = mixed[p]
                        if add:
                            value = value + target[2 * i + p, here, lanes]
                        target[2 * i + p, here, lanes] = value
            return carry

        lax.fori_loop(0, size_x // 2, step, 0)


def body(
    noise_level0,
    noise_level1,
    noise_level2,
    noise_level3,
    noise_level4,
    refine_kernels,
    noise_kernels,
    cotangent,
):
    noises = (noise_level0, noise_level1, noise_level2, noise_level3, noise_level4)
    plan = Plan([noise.shape for noise in noises])
    nx, ny = plan.pairs[LEVELS]
    rows = plan.rows[LEVELS]
    vmem = pl.BlockSpec(memory_space=pltpu.VMEM)
    smem = pl.BlockSpec(memory_space=pltpu.SMEM)
    anywhere = pl.BlockSpec(memory_space=pl.ANY)

    def scratch(*shape):
        return pltpu.VMEM(shape, F32)

    def field_shape(level):
        grown = plan.ext[level]
        return (grown[0], grown[1] + 8, 128)

    messages = [scratch(plan.message_rows, 128)] * 4
    count = len(DIRS)
    fine, grad0, grad1, grad2, grad3 = pl.pallas_call(
        lambda *refs: main_kernel(plan, *refs),
        out_shape=[jax.ShapeDtypeStruct((2, 2 * nx, rows, 128), F32)]
        + [jax.ShapeDtypeStruct(noise.shape, F32) for noise in noises[:LEVELS]],
        in_specs=[vmem] * 4 + [smem] * 2 + [anywhere],
        out_specs=[vmem] * 5,
        scratch_shapes=[scratch(*shape) for shape in plan.ext]
        + [scratch(*shape) for shape in plan.ext]
        + [scratch(*field_shape(level)) for level in (1, 2, 3)]
        + [scratch(*plan.ext[level]) for level in (1, 2, 3)]
        + [
            scratch(LEVELS, 108, 8, 128),
            scratch(LEVELS - 1, 16, 8, 128),
            scratch(LEVELS - 1, 16, 8, 128),
            scratch(*cotangent.shape),
            scratch(8, 128),
            scratch(3, nx + 2, 2 * up8(ny + 2), 128),
            scratch(2, 2 * nx, rows, 128),
            scratch(2, 2 * nx, rows, 128),
            scratch(9, nx + 2, rows, 128),
            scratch(3, rows + 16, 128),
        ]
        + messages
        + [pltpu.SemaphoreType.DMA((4,))]
        + [pltpu.SemaphoreType.DMA((count,))] * 4,
        compiler_params=pltpu.CompilerParams(
            collective_id=0, has_side_effects=True, vmem_limit_bytes=32 * 1024 * 1024
        ),
    )(*noises[:LEVELS], refine_kernels, noise_kernels, cotangent)

    steps = 4
    size_x, size_y, size_z = noise_level4.shape
    block = pl.BlockSpec((size_x // steps, size_y, size_z), lambda i: (i, 0, 0))
    whole = [pl.BlockSpec(noise.shape, lambda i: (0, 0, 0)) for noise in noises[:LEVELS]]
    density, grad4, *small = pl.pallas_call(
        finish_kernel,
        grid=(steps,),
        out_shape=[jax.ShapeDtypeStruct(noise_level4.shape, F32)] * 2
        + [jax.ShapeDtypeStruct(noise.shape, F32) for noise in noises[:LEVELS]],
        in_specs=[
            pl.BlockSpec((2, size_x // steps, rows, 128), lambda i: (0, i, 0, 0)),
            block,
            block,
            smem,
        ]
        + whole,
        out_specs=[block, block] + whole,
        scratch_shapes=[scratch(16, 8, 128), scratch(16, 8, 128)],
        compiler_params=pltpu.CompilerParams(vmem_limit_bytes=32 * 1024 * 1024),
    )(fine, noise_level4, cotangent, noise_kernels, grad0, grad1, grad2, grad3)
    return (density, *small[:1], *small[1:], grad4)


def solution(mesh):
    placed = P("group", "brick", None)
    return jax.shard_map(
        body,
        mesh=mesh,
        in_specs=(placed,) * 5 + (P(), P(), placed),
        out_specs=(placed,) * 6,
        check_vma=False,
    )
```

```python
import jax
import jax.numpy as jnp
from jax import lax
from jax.experimental import pallas as pl
from jax.experimental.pallas import tpu as pltpu
from jax.sharding import PartitionSpec as P

LEVELS = 4
F32 = jnp.float32
BF16 = jnp.bfloat16
MESH = pl.DeviceIdType.MESH

NEAR = [(dx, dy) for dx in (-1, 0, 1) for dy in (-1, 0, 1) if (dx, dy) != (0, 0)]
FAR = [(dx, dy) for dx in (-2, 2) for dy in (-1, 0, 1)]
DIRS = NEAR + FAR


def up8(n):
    return -(-n // 8) * 8


class Plan:
    def __init__(self, shapes):
        self.block = shapes
        self.pairs = {}
        for level in range(1, LEVELS + 1):
            grow = 0 if level == LEVELS else 2
            self.pairs[level] = (shapes[level][0] // 2 + grow, shapes[level][1] // 2 + grow)
        self.rows = {level: up8(2 * ny) for level, (_, ny) in self.pairs.items()}
        self.ext = [
            (shapes[level][0] + 4, up8(shapes[level][1] + 4), 128) for level in range(LEVELS)
        ]
        self.pieces = {}
        self.offset = {}
        total = 0
        for dx, dy in DIRS:
            rows = 0
            pieces = []
            for level in range(LEVELS):
                if abs(dx) == 2 and level > 0:
                    continue
                bx, by = shapes[level][0], shapes[level][1]
                count_x = bx if dx == 0 else min(2, bx)
                count_y = by if dy == 0 else 2
                pieces.append((level, rows, count_x, count_y))
                rows += count_x * count_y
            self.pieces[dx, dy] = pieces
            self.offset[dx, dy] = (total, up8(rows))
            total += up8(rows)
        self.message_rows = total


def inner(step, size):
    if step == 0 or size == 1:
        return 2
    return 2 if step < 0 else size


def outer(step, size):
    if step == 0:
        return 2
    if size == 1:
        return 2 + step
    return 0 if step < 0 else size + 2


def lane_iota(shape):
    return lax.broadcasted_iota(jnp.int32, shape, len(shape) - 1)


def row_iota(shape):
    return lax.broadcasted_iota(jnp.int32, shape, len(shape) - 2)


def split(values):
    high = values.astype(BF16)
    return high, (values - high.astype(F32)).astype(BF16)


def select_dot(values, matrix):
    high, low = split(values)
    return jnp.dot(high, matrix, preferred_element_type=F32) + jnp.dot(
        low, matrix, preferred_element_type=F32
    )


def merge_matrix(size, width):
    row, col = row_iota((256, width)), lane_iota((256, width))
    parity = (row >= 128).astype(jnp.int32)
    at = row - 128 * parity
    return jnp.where((col == 2 * at + parity) & (at < size), 1.0, 0.0).astype(BF16)


def part_matrix(size, width):
    row, col = row_iota((width, 256)), lane_iota((width, 256))
    parity = (col >= 128).astype(jnp.int32)
    at = col - 128 * parity
    return jnp.where((row == 2 * at + parity) & (at < size), 1.0, 0.0).astype(BF16)


def parities():
    shape = (8, 128)
    return row_iota(shape) % 2 == 0, lane_iota(shape) % 2 == 0


def noise_patterns(read, store, transpose):
    even_row, even_lane = parities()
    for p in range(2):
        for other in range(2):
            for dq in range(2):
                for dr in range(2):
                    value = {}
                    for q in range(2):
                        for r in range(2):
                            here = 4 * p + 2 * q + r
                            there = 4 * other + 2 * (q ^ dq) + (r ^ dr)
                            value[q, r] = read(there, here) if transpose else read(here, there)
                    store(
                        p * 8 + other * 4 + dq * 2 + dr,
                        jnp.where(
                            even_row,
                            jnp.where(even_lane, value[0, 0], value[0, 1]),
                            jnp.where(even_lane, value[1, 0], value[1, 1]),
                        ),
                    )


def swaps(tile):
    even_row, even_lane = parities()

    def lanes(v):
        return jnp.where(even_lane, pltpu.roll(v, 127, 1), pltpu.roll(v, 1, 1))

    turned = jnp.where(even_row, pltpu.roll(tile, 7, 0), pltpu.roll(tile, 1, 0))
    return [tile, lanes(tile), turned, lanes(turned)]


def mix(first, second, weights):
    terms = swaps(first) + swaps(second)
    results = []
    for p in range(2):
        total = weights[p * 8] * terms[0]
        for at in range(1, 8):
            total = total + weights[p * 8 + at] * terms[at]
        results.append(total)
    return results


def shift_down(values, size):
    lane = lane_iota(values.shape)
    return jnp.where((lane > 0) & (lane < size), pltpu.roll(values, 1, 1), 0.0)


def shift_up(values, size):
    lane = lane_iota(values.shape)
    return jnp.where(lane < size - 1, pltpu.roll(values, 127, 1), 0.0)


def loop(count, step, unroll):
    if unroll >= count:
        for i in range(count):
            step(i)
        return

    def one(i, carry):
        step(i)
        return carry

    lax.fori_loop(0, count, one, 0, unroll=unroll)


UNROLL_MAIN = {1: 8, 2: 8, 3: 8, 4: 1}
UNROLL_SIDE = {1: 16, 2: 16, 3: 16, 4: 16}
UNROLL_MIX = {1: 16, 2: 16, 3: 16, 4: 1}


def main_kernel(
    plan,
    noise0, noise1, noise2, noise3, noise4, refine_hbm, noise_hbm, cotangent,
    density, grad0, grad1, grad2, grad3, grad4,
    own0, own1, own2, own3, refine_k, noise_k,
    ext0, ext1, ext2, ext3, part0, part1, part2, part3,
    field1, field2, field3, grads1, grads2, grads3,
    taps1, taps2, taps3, taps4,
    pattern, mixing, mixing_t, merges, parts, merge_last, part_last,
    cot, excite, spread, sums, turned,
    send_a, recv_a, send_b, recv_b,
    own_sem, table_sem, cot_sem, excite_sem,
    send_a_sem, recv_a_sem, send_b_sem, recv_b_sem,
):
    group, brick = lax.axis_index("group"), lax.axis_index("brick")
    groups, bricks = lax.axis_size("group"), lax.axis_size("brick")
    ext = [ext0, ext1, ext2, ext3]
    part = [part0, part1, part2, part3]
    field = [ext0, field1, field2, field3]
    grads = [part0, grads1, grads2, grads3]
    taps = [None, taps1, taps2, taps3, taps4]

    def neighbour(dx, dy):
        return (
            lax.rem(group + (dx + groups), groups),
            lax.rem(brick + (dy + bricks), bricks),
        )

    own = [own0, own1, own2, own3]
    own_copies = []
    for at, source in enumerate((noise0, noise1, noise2, noise3)):
        own_copies.append(pltpu.make_async_copy(source, own[at], own_sem.at[at]))
    table_copies = [
        pltpu.make_async_copy(refine_hbm, refine_k, table_sem.at[0]),
        pltpu.make_async_copy(noise_hbm, noise_k, table_sem.at[1]),
    ]
    cot_chunks = cot_sem.shape[0]
    chunk = cot.shape[0] // cot_chunks
    cot_copies = [
        pltpu.make_async_copy(
            cotangent.at[pl.ds(at * chunk, chunk)], cot.at[pl.ds(at * chunk, chunk)], cot_sem.at[at]
        )
        for at in range(cot_chunks)
    ]
    excite_copy = pltpu.make_async_copy(noise4, excite, excite_sem.at[0])
    for copy in own_copies + table_copies + cot_copies + [excite_copy]:
        copy.start()

    barrier = pltpu.get_barrier_semaphore()
    for dx, dy in DIRS:
        pl.semaphore_signal(barrier, inc=1, device_id=neighbour(dx, dy), device_id_type=MESH)

    for level in range(LEVELS):
        ext[level][...] = jnp.zeros(ext[level].shape, F32)
        if level:
            grads[level][...] = jnp.zeros(grads[level].shape, F32)
        part[level][...] = jnp.zeros(part[level].shape, F32)
    send_a[...] = jnp.zeros(send_a.shape, F32)
    send_b[...] = jnp.zeros(send_b.shape, F32)
    for level in range(1, LEVELS + 1):
        nx, _ = plan.pairs[level]
        rows = plan.rows[level]
        for t in range(3):
            for x in range(nx + 2):
                taps[level][t, x, 0:8, :] = jnp.zeros((8, 128), F32)
                taps[level][t, x, 8 + rows : 16 + rows, :] = jnp.zeros((8, 128), F32)
            for x in (0, nx + 1):
                taps[level][t, x, 8 : 8 + rows, :] = jnp.zeros((rows, 128), F32)
        size = plan.block[level][2] // 2
        if level < LEVELS:
            merges[level - 1] = merge_matrix(size, 128)
            parts[level - 1] = part_matrix(size, 128)
        else:
            merge_last[...] = merge_matrix(size, 256)
            part_last[...] = part_matrix(size, 256)
    for level in range(LEVELS):
        bx, by, size = plan.block[level]
        own_copies[level].wait()
        ext[level][2 : 2 + bx, 2 : 2 + by, 0:size] = own[level][...]

    def pack(source, target, start_of, sign):
        for dx, dy in DIRS:
            base, _ = plan.offset[dx, dy]
            for level, row, count_x, count_y in plan.pieces[dx, dy]:
                bx, by, _ = plan.block[level]
                x0, y0 = start_of(sign * dx, bx), start_of(sign * dy, by)
                for i in range(count_x):
                    target[pl.ds(base + row + i * count_y, count_y), :] = source[level][
                        x0 + i, y0 : y0 + count_y, :
                    ]

    def unpack(source, target, start_of, add):
        for dx, dy in DIRS:
            base, _ = plan.offset[dx, dy]
            for level, row, count_x, count_y in plan.pieces[dx, dy]:
                bx, by, _ = plan.block[level]
                x0, y0 = start_of(-dx, bx), start_of(-dy, by)
                for i in range(count_x):
                    value = source[pl.ds(base + row + i * count_y, count_y), :]
                    if add:
                        value = value + target[level][x0 + i, y0 : y0 + count_y, :]
                    target[level][x0 + i, y0 : y0 + count_y, :] = value

    def copies(source, target, send_sem, recv_sem):
        made = []
        for at, (dx, dy) in enumerate(DIRS):
            base, rows = plan.offset[dx, dy]
            made.append(
                pltpu.make_async_remote_copy(
                    src_ref=source.at[pl.ds(base, rows)],
                    dst_ref=target.at[pl.ds(base, rows)],
                    send_sem=send_sem.at[at],
                    recv_sem=recv_sem.at[at],
                    device_id=neighbour(dx, dy),
                    device_id_type=MESH,
                )
            )
        return made

    pack(ext, send_a, inner, 1)
    for copy in table_copies:
        copy.wait()

    even_row, _ = parities()

    def build(level, carry):
        for o in range(27):
            for p in range(2):
                for r in range(2):
                    pattern[level, o * 4 + p * 2 + r] = jnp.where(
                        even_row,
                        refine_k[level, 4 * p + r, o],
                        refine_k[level, 4 * p + 2 + r, o],
                    )

        def read(u, v):
            return noise_k[level, u, v]

        def store(at, value):
            mixing[level, at] = value

        def store_t(at, value):
            mixing_t[level, at] = value

        noise_patterns(read, store, False)
        noise_patterns(read, store_t, True)
        return carry

    lax.fori_loop(0, LEVELS, build, 0)

    def inside(level, x_at, shape, first_row, first_x):
        bx, by, _ = plan.block[level]
        y = row_iota(shape) + (brick * by - 2 + first_row)
        x = group * bx - 2 + first_x + x_at
        limit = jnp.where((x >= 0) & (x < groups * bx), bricks * by, 0)
        return (y >= 0) & (y < limit)

    def tile_rows(at):
        return pl.ds(8 * at, 8)

    def adjoint(level):
        nx, ny = plan.pairs[level]
        rows = plan.rows[level]
        size = plan.block[level][2] // 2
        tiles = rows // 8
        tap = taps[level]

        def store_parts(both, x0, count):
            for r in range(2):
                flat = both[:, 128 * r : 128 * (r + 1)]
                for w, moved in enumerate((shift_up(flat, size), flat, shift_down(flat, size))):
                    turned[w, r, x0 : x0 + count, 0:rows, :] = moved.reshape(count, rows, 128)

        if level == LEVELS:
            for at in range(cot_chunks):
                cot_copies[at].wait()
                flat = cot[at * chunk : (at + 1) * chunk].reshape(chunk * rows, 256)
                store_parts(select_dot(flat, part_last[...]), at * chunk, chunk)
        else:
            flat = grads[level][:, 0:rows, :].reshape(2 * nx * rows, 128)
            store_parts(select_dot(flat, parts[level - 1]), 0, 2 * nx)

        for s in (1, 0, 2):
            weights = [pattern[level - 1, s * 36 + at] for at in range(36)]

            def step(i):
                for tile in range(tiles):
                    here = tile_rows(tile)
                    there = pl.ds(8 + 8 * tile, 8)
                    values = [
                        turned[w, r, 2 * i + p, here, :]
                        for w in range(3)
                        for p in range(2)
                        for r in range(2)
                    ]
                    for t in range(3):
                        total = weights[12 * t] * values[0]
                        for at in range(1, 12):
                            total = total + weights[12 * t + at] * values[at]
                        if s != 1:
                            total = total + tap[t, i + s, there, :]
                        tap[t, i + s, there, :] = total

            loop(nx, step, UNROLL_MAIN[level])

        target = grads[level - 1]
        first = 1 if level == LEVELS else 0

        def combine(x):
            total = None
            for t in range(3):
                for q in range(2):
                    value = tap[t, x, pl.ds(8 - 2 * t + q, ny + 2, stride=2), :]
                    total = value if total is None else total + value
            keep = inside(level - 1, x, (ny + 2, 128), first, first)
            target[x + first, first : first + ny + 2, :] = jnp.where(keep, total, 0.0)

        loop(nx + 2, combine, UNROLL_SIDE[level])

    def mix_level(level, source, target, weights_of, masked):
        nx, _ = plan.pairs[level]
        weights = [weights_of[level - 1, at] for at in range(16)]
        halves = source.shape[2] // 128

        def step(i):
            for tile in range(plan.rows[level] // 8):
                for half in range(halves):
                    here, lanes = tile_rows(tile), pl.ds(128 * half, 128)
                    mixed = mix(
                        source[2 * i, here, lanes], source[2 * i + 1, here, lanes], weights
                    )
                    for p in range(2):
                        value = mixed[p]
                        if masked:
                            value = value + target[2 * i + p, here, lanes]
                            keep = inside(level, 2 * i + p, (8, 128), 8 * tile, 0)
                            value = jnp.where(keep, value, 0.0)
                        target[2 * i + p, here, lanes] = value

        loop(nx, step, UNROLL_MIX[level])

    adjoint(LEVELS)
    pl.semaphore_wait(barrier, len(DIRS))
    out_a = copies(send_a, recv_a, send_a_sem, recv_a_sem)
    for copy in out_a:
        copy.start()

    for level in range(LEVELS - 1, 0, -1):
        mix_level(level, grads[level], part[level], mixing_t, False)
        adjoint(level)

    pack(part, send_b, outer, 1)
    out_b = copies(send_b, recv_b, send_b_sem, recv_b_sem)
    for copy in out_b:
        copy.start()
    mix_level(LEVELS, cot, grad4, mixing_t, False)
    excite_copy.wait()
    mix_level(LEVELS, excite, density, mixing, False)

    for copy in out_a:
        copy.wait_recv()
    unpack(recv_a, ext, outer, False)
    for x in range(ext0.shape[0]):
        keep = inside(0, x, ext0.shape[1:], 0, 0)
        ext0[x] = jnp.where(keep, ext0[x], 0.0)

    def forward(level):
        nx, ny = plan.pairs[level]
        rows = plan.rows[level]
        size = plan.block[level][2] // 2
        first = 1 if level == LEVELS else 0
        source = field[level - 1]
        count = up8(ny + 2)

        def widen(x):
            for tile in range(count // 8):
                value = source[x + first, pl.ds(first + 8 * tile, 8), :]
                for w, moved in enumerate((shift_down(value, size), value, shift_up(value, size))):
                    for q in range(2):
                        spread[w, x, pl.ds(16 * tile + q, 8, stride=2), :] = moved

        loop(nx + 2, widen, UNROLL_SIDE[level])

        for s in range(3):
            weights = [pattern[level - 1, s * 36 + at] for at in range(36)]

            def step(i):
                for tile in range(rows // 8):
                    here = tile_rows(tile)
                    totals = [None] * 4
                    for tap in range(9):
                        value = spread[tap % 3, i + s, pl.ds(8 * tile + 2 * (tap // 3), 8), :]
                        for at in range(4):
                            term = weights[tap * 4 + at] * value
                            totals[at] = term if totals[at] is None else totals[at] + term
                    for at in range(4):
                        p, r = at // 2, at % 2
                        value = totals[at]
                        if s:
                            value = value + sums[r, 2 * i + p, here, :]
                        sums[r, 2 * i + p, here, :] = value

            loop(nx, step, UNROLL_MAIN[level])

        def merged(x0, count_x, matrix):
            both = jnp.concatenate(
                [sums[r, x0 : x0 + count_x, 0:rows, :].reshape(count_x * rows, 128) for r in range(2)],
                axis=1,
            )
            return select_dot(both, matrix).reshape(count_x, rows, -1)

        if level < LEVELS:
            field[level][:, 0:rows, :] = merged(0, 2 * nx, merges[level - 1])
            mix_level(level, ext[level], field[level], mixing, True)
        else:
            for at in range(cot_chunks):
                here = slice(at * chunk, (at + 1) * chunk)
                density[here] = density[here] + merged(at * chunk, chunk, merge_last[...])

    for level in range(1, LEVELS + 1):
        forward(level)

    for copy in out_b:
        copy.wait_recv()
    unpack(recv_b, part, inner, True)
    for level, target in enumerate((grad0, grad1, grad2, grad3)):
        bx, by, size = plan.block[level]
        target[...] = part[level][2 : 2 + bx, 2 : 2 + by, 0:size]
    for copy in out_a + out_b:
        copy.wait_send()


def finish_kernel(*refs):
    count = (len(refs) - 1) // 2
    copies = [
        pltpu.make_async_copy(refs[at], refs[count + at], refs[-1].at[at]) for at in range(count)
    ]
    for copy in copies:
        copy.start()
    for copy in copies:
        copy.wait()


def pin(array):
    return pltpu.with_memory_space_constraint(array, pltpu.HBM)


def body(
    noise_level0,
    noise_level1,
    noise_level2,
    noise_level3,
    noise_level4,
    refine_kernels,
    noise_kernels,
    cotangent,
):
    noises = (noise_level0, noise_level1, noise_level2, noise_level3, noise_level4)
    plan = Plan([noise.shape for noise in noises])
    nx, ny = plan.pairs[LEVELS]
    rows = plan.rows[LEVELS]
    hbm = pl.BlockSpec(memory_space=pltpu.HBM)
    vmem = pl.BlockSpec(memory_space=pltpu.VMEM)
    size_z = noise_level4.shape[2]

    def scratch(*shape, dtype=F32):
        return pltpu.VMEM(shape, dtype)

    def field_shape(level):
        grown = plan.ext[level]
        return (grown[0], grown[1] + 8, 128)

    count = len(DIRS)
    dma = pltpu.SemaphoreType.DMA
    results = [
        jax.ShapeDtypeStruct(array.shape, F32)
        for array in (noise_level4, *noises[:LEVELS], cotangent)
    ]
    blocks = pl.pallas_call(
        lambda *refs: main_kernel(plan, *refs),
        out_shape=results,
        in_specs=[hbm] * 8,
        out_specs=[vmem] * 6,
        scratch_shapes=[scratch(*noise.shape) for noise in noises[:LEVELS]]
        + [pltpu.SMEM(table.shape, F32) for table in (refine_kernels, noise_kernels)]
        + [scratch(*shape) for shape in plan.ext]
        + [scratch(*shape) for shape in plan.ext]
        + [scratch(*field_shape(level)) for level in (1, 2, 3)]
        + [scratch(*plan.ext[level]) for level in (1, 2, 3)]
        + [
            scratch(3, plan.pairs[level][0] + 2, plan.rows[level] + 16, 128)
            for level in (1, 2, 3, 4)
        ]
        + [
            scratch(LEVELS, 108, 8, 128),
            scratch(LEVELS, 16, 8, 128),
            scratch(LEVELS, 16, 8, 128),
            scratch(LEVELS - 1, 256, 128, dtype=BF16),
            scratch(LEVELS - 1, 128, 256, dtype=BF16),
            scratch(256, size_z, dtype=BF16),
            scratch(size_z, 256, dtype=BF16),
            scratch(*cotangent.shape),
            scratch(*noise_level4.shape),
            scratch(3, nx + 2, 2 * up8(ny + 2), 128),
            scratch(2, 2 * nx, rows, 128),
            scratch(3, 2, 2 * nx, rows, 128),
        ]
        + [scratch(plan.message_rows, 128)] * 4
        + [dma((LEVELS,)), dma((2,)), dma((4,)), dma((1,))]
        + [dma((count,))] * 4,
        compiler_params=pltpu.CompilerParams(
            collective_id=0, has_side_effects=True, vmem_limit_bytes=32 * 1024 * 1024
        ),
    )(*[pin(noise) for noise in noises], pin(refine_kernels), pin(noise_kernels), pin(cotangent))

    return pl.pallas_call(
        finish_kernel,
        out_shape=[pltpu.HBM(result.shape, F32) for result in results],
        in_specs=[vmem] * 6,
        out_specs=[hbm] * 6,
        scratch_shapes=[dma((6,))],
        compiler_params=pltpu.CompilerParams(vmem_limit_bytes=8 * 1024 * 1024),
    )(*blocks)


def solution(mesh):
    placed = P("group", "brick", None)
    return jax.shard_map(
        body,
        mesh=mesh,
        in_specs=(placed,) * 5 + (P(), P(), placed),
        out_specs=(placed,) * 6,
        check_vma=False,
    )
```

```python
import jax
import jax.numpy as jnp
from jax import lax
from jax.experimental import pallas as pl
from jax.experimental.pallas import tpu as pltpu
from jax.sharding import PartitionSpec as P

LEVELS = 4
F32 = jnp.float32
BF16 = jnp.bfloat16
MESH = pl.DeviceIdType.MESH

NEAR = [(dx, dy) for dx in (-1, 0, 1) for dy in (-1, 0, 1) if (dx, dy) != (0, 0)]
FAR = [(dx, dy) for dx in (-2, 2) for dy in (-1, 0, 1)]
DIRS = NEAR + FAR


def up8(n):
    return -(-n // 8) * 8


class Plan:
    def __init__(self, shapes):
        self.block = shapes
        self.pairs = {}
        for level in range(1, LEVELS + 1):
            grow = 0 if level == LEVELS else 2
            self.pairs[level] = (shapes[level][0] // 2 + grow, shapes[level][1] // 2 + grow)
        self.rows = {level: up8(2 * ny) for level, (_, ny) in self.pairs.items()}
        self.ext = [
            (shapes[level][0] + 4, up8(shapes[level][1] + 4), 128) for level in range(LEVELS)
        ]
        self.pieces = {}
        self.offset = {}
        total = 0
        for dx, dy in DIRS:
            rows = 0
            pieces = []
            for level in range(LEVELS):
                if abs(dx) == 2 and level > 0:
                    continue
                bx, by = shapes[level][0], shapes[level][1]
                count_x = bx if dx == 0 else min(2, bx)
                count_y = by if dy == 0 else 2
                pieces.append((level, rows, count_x, count_y))
                rows += count_x * count_y
            self.pieces[dx, dy] = pieces
            self.offset[dx, dy] = (total, up8(rows))
            total += up8(rows)
        self.message_rows = total


def inner(step, size):
    if step == 0 or size == 1:
        return 2
    return 2 if step < 0 else size


def outer(step, size):
    if step == 0:
        return 2
    if size == 1:
        return 2 + step
    return 0 if step < 0 else size + 2


def lane_iota(shape):
    return lax.broadcasted_iota(jnp.int32, shape, len(shape) - 1)


def row_iota(shape):
    return lax.broadcasted_iota(jnp.int32, shape, len(shape) - 2)


def split(values):
    high = values.astype(BF16)
    return high, (values - high.astype(F32)).astype(BF16)


def select_dot(values, matrix):
    high, low = split(values)
    return jnp.dot(high, matrix, preferred_element_type=F32) + jnp.dot(
        low, matrix, preferred_element_type=F32
    )


def merge_matrix(size, width):
    row, col = row_iota((256, width)), lane_iota((256, width))
    parity = (row >= 128).astype(jnp.int32)
    at = row - 128 * parity
    return jnp.where((col == 2 * at + parity) & (at < size), 1.0, 0.0).astype(BF16)


def part_matrix(size, width):
    row, col = row_iota((width, 256)), lane_iota((width, 256))
    parity = (col >= 128).astype(jnp.int32)
    at = col - 128 * parity
    return jnp.where((row == 2 * at + parity) & (at < size), 1.0, 0.0).astype(BF16)


def parities():
    shape = (8, 128)
    return row_iota(shape) % 2 == 0, lane_iota(shape) % 2 == 0


def noise_patterns(read, store, transpose):
    even_row, even_lane = parities()
    for p in range(2):
        for other in range(2):
            for dq in range(2):
                for dr in range(2):
                    value = {}
                    for q in range(2):
                        for r in range(2):
                            here = 4 * p + 2 * q + r
                            there = 4 * other + 2 * (q ^ dq) + (r ^ dr)
                            value[q, r] = read(there, here) if transpose else read(here, there)
                    store(
                        p * 8 + other * 4 + dq * 2 + dr,
                        jnp.where(
                            even_row,
                            jnp.where(even_lane, value[0, 0], value[0, 1]),
                            jnp.where(even_lane, value[1, 0], value[1, 1]),
                        ),
                    )


def swaps(tile):
    even_row, even_lane = parities()

    def lanes(v):
        return jnp.where(even_lane, pltpu.roll(v, 127, 1), pltpu.roll(v, 1, 1))

    turned = jnp.where(even_row, pltpu.roll(tile, 7, 0), pltpu.roll(tile, 1, 0))
    return [tile, lanes(tile), turned, lanes(turned)]


def mix(first, second, weights):
    terms = swaps(first) + swaps(second)
    results = []
    for p in range(2):
        total = weights[p * 8] * terms[0]
        for at in range(1, 8):
            total = total + weights[p * 8 + at] * terms[at]
        results.append(total)
    return results


def shift_down(values, size):
    lane = lane_iota(values.shape)
    return jnp.where((lane > 0) & (lane < size), pltpu.roll(values, 1, 1), 0.0)


def shift_up(values, size):
    lane = lane_iota(values.shape)
    return jnp.where(lane < size - 1, pltpu.roll(values, 127, 1), 0.0)


def loop(count, step, unroll):
    if unroll >= count:
        for i in range(count):
            step(i)
        return

    def one(i, carry):
        step(i)
        return carry

    lax.fori_loop(0, count, one, 0, unroll=unroll)


UNROLL_MAIN = {1: 8, 2: 8, 3: 8, 4: 1}
UNROLL_SIDE = {1: 16, 2: 16, 3: 16, 4: 16}
UNROLL_MIX = {1: 16, 2: 16, 3: 16, 4: 2}
LINE = 8


def main_kernel(
    plan,
    noise0, noise1, noise2, noise3, noise4, refine_hbm, noise_hbm, cotangent,
    density, grad0, grad1, grad2, grad3, grad4,
    own0, own1, own2, own3, refine_k, noise_k,
    ext0, ext1, ext2, ext3, part0, part1, part2, part3,
    field1, field2, field3, grads1, grads2, grads3,
    taps1, taps2, taps3, taps4,
    pattern, mixing, mixing_t, merges, parts, merge_last, part_last,
    cot, excite, spread, sums, turned,
    send_a, recv_a, send_b, recv_b,
    own_sem, table_sem, cot_sem, excite_sem,
    send_a_sem, recv_a_sem, send_b_sem, recv_b_sem,
):
    group, brick = lax.axis_index("group"), lax.axis_index("brick")
    groups, bricks = lax.axis_size("group"), lax.axis_size("brick")
    ext = [ext0, ext1, ext2, ext3]
    part = [part0, part1, part2, part3]
    field = [ext0, field1, field2, field3]
    grads = [part0, grads1, grads2, grads3]
    taps = [None, taps1, taps2, taps3, taps4]

    def neighbour(dx, dy):
        return (
            lax.rem(group + (dx + groups), groups),
            lax.rem(brick + (dy + bricks), bricks),
        )

    own = [own0, own1, own2, own3]
    own_copies = []
    for at, source in enumerate((noise0, noise1, noise2, noise3)):
        own_copies.append(pltpu.make_async_copy(source, own[at], own_sem.at[at]))
    table_copies = [
        pltpu.make_async_copy(refine_hbm, refine_k, table_sem.at[0]),
        pltpu.make_async_copy(noise_hbm, noise_k, table_sem.at[1]),
    ]
    cot_chunks = cot_sem.shape[0]
    chunk = cot.shape[0] // cot_chunks
    cot_copies = [
        pltpu.make_async_copy(
            cotangent.at[pl.ds(at * chunk, chunk)], cot.at[pl.ds(at * chunk, chunk)], cot_sem.at[at]
        )
        for at in range(cot_chunks)
    ]
    excite_copy = pltpu.make_async_copy(noise4, excite, excite_sem.at[0])
    for copy in own_copies + table_copies + cot_copies + [excite_copy]:
        copy.start()

    def exists(dx, dy):
        x, y = group + dx, brick + dy
        return (x >= 0) & (x < groups) & (y >= 0) & (y < bricks)

    recv_a[...] = jnp.zeros(recv_a.shape, F32)
    recv_b[...] = jnp.zeros(recv_b.shape, F32)
    barrier = pltpu.get_barrier_semaphore()
    partners = 0
    for dx, dy in DIRS:
        partners = partners + exists(dx, dy).astype(jnp.int32)

        @pl.when(exists(dx, dy))
        def _():
            pl.semaphore_signal(barrier, inc=1, device_id=neighbour(dx, dy), device_id_type=MESH)

    for level in range(LEVELS):
        ext[level][...] = jnp.zeros(ext[level].shape, F32)
        if level:
            grads[level][...] = jnp.zeros(grads[level].shape, F32)
        part[level][...] = jnp.zeros(part[level].shape, F32)
    send_a[...] = jnp.zeros(send_a.shape, F32)
    send_b[...] = jnp.zeros(send_b.shape, F32)
    for level in range(1, LEVELS + 1):
        nx, _ = plan.pairs[level]
        rows = plan.rows[level]
        for t in range(3):
            for x in range(nx + 2):
                taps[level][t, x, 0:8, :] = jnp.zeros((8, 128), F32)
                taps[level][t, x, 8 + rows : 16 + rows, :] = jnp.zeros((8, 128), F32)
            for x in (0, nx + 1):
                taps[level][t, x, 8 : 8 + rows, :] = jnp.zeros((rows, 128), F32)
        size = plan.block[level][2] // 2
        if level < LEVELS:
            merges[level - 1] = merge_matrix(size, 128)
            parts[level - 1] = part_matrix(size, 128)
        else:
            merge_last[...] = merge_matrix(size, 256)
            part_last[...] = part_matrix(size, 256)
    for level in range(LEVELS):
        bx, by, size = plan.block[level]
        own_copies[level].wait()
        ext[level][2 : 2 + bx, 2 : 2 + by, 0:size] = own[level][...]

    def pack(source, target, start_of, sign):
        for dx, dy in DIRS:
            base, _ = plan.offset[dx, dy]
            for level, row, count_x, count_y in plan.pieces[dx, dy]:
                bx, by, _ = plan.block[level]
                x0, y0 = start_of(sign * dx, bx), start_of(sign * dy, by)
                for i in range(count_x):
                    target[pl.ds(base + row + i * count_y, count_y), :] = source[level][
                        x0 + i, y0 : y0 + count_y, :
                    ]

    def unpack(source, target, start_of, add):
        for dx, dy in DIRS:
            base, _ = plan.offset[dx, dy]
            for level, row, count_x, count_y in plan.pieces[dx, dy]:
                bx, by, _ = plan.block[level]
                x0, y0 = start_of(-dx, bx), start_of(-dy, by)
                for i in range(count_x):
                    value = source[pl.ds(base + row + i * count_y, count_y), :]
                    if add:
                        value = value + target[level][x0 + i, y0 : y0 + count_y, :]
                    target[level][x0 + i, y0 : y0 + count_y, :] = value

    def copies(source, target, send_sem, recv_sem):
        made = []
        for at, (dx, dy) in enumerate(DIRS):
            base, rows = plan.offset[dx, dy]
            made.append(
                pltpu.make_async_remote_copy(
                    src_ref=source.at[pl.ds(base, rows)],
                    dst_ref=target.at[pl.ds(base, rows)],
                    send_sem=send_sem.at[at],
                    recv_sem=recv_sem.at[at],
                    device_id=neighbour(dx, dy),
                    device_id_type=MESH,
                )
            )
        return made

    def start_all(made):
        for (dx, dy), copy in zip(DIRS, made):
            pl.when(exists(dx, dy))(copy.start)

    def wait_sent(made):
        for (dx, dy), copy in zip(DIRS, made):
            pl.when(exists(dx, dy))(copy.wait_send)

    def wait_received(made):
        for (dx, dy), copy in zip(DIRS, made):
            pl.when(exists(-dx, -dy))(copy.wait_recv)

    pack(ext, send_a, inner, 1)
    out_a = copies(send_a, recv_a, send_a_sem, recv_a_sem)
    out_b = copies(send_b, recv_b, send_b_sem, recv_b_sem)
    first_row = lax.rem(brick, LINE) == 0

    @pl.when(jnp.logical_not(first_row))
    def _():
        pl.semaphore_wait(barrier, partners)
        start_all(out_a)

    for copy in table_copies:
        copy.wait()

    even_row, _ = parities()

    def build(level, carry):
        for o in range(27):
            for p in range(2):
                for r in range(2):
                    pattern[level, o * 4 + p * 2 + r] = jnp.where(
                        even_row,
                        refine_k[level, 4 * p + r, o],
                        refine_k[level, 4 * p + 2 + r, o],
                    )

        def read(u, v):
            return noise_k[level, u, v]

        def store(at, value):
            mixing[level, at] = value

        def store_t(at, value):
            mixing_t[level, at] = value

        noise_patterns(read, store, False)
        noise_patterns(read, store_t, True)
        return carry

    lax.fori_loop(0, LEVELS, build, 0)

    def inside(level, x_at, shape, first_row, first_x):
        bx, by, _ = plan.block[level]
        y = row_iota(shape) + (brick * by - 2 + first_row)
        x = group * bx - 2 + first_x + x_at
        limit = jnp.where((x >= 0) & (x < groups * bx), bricks * by, 0)
        return (y >= 0) & (y < limit)

    def tile_rows(at):
        return pl.ds(8 * at, 8)

    def adjoint(level):
        nx, ny = plan.pairs[level]
        rows = plan.rows[level]
        size = plan.block[level][2] // 2
        tiles = rows // 8
        tap = taps[level]

        def store_parts(both, x0, count):
            for r in range(2):
                flat = both[:, 128 * r : 128 * (r + 1)]
                for w, moved in enumerate((shift_up(flat, size), flat, shift_down(flat, size))):
                    turned[w, r, x0 : x0 + count, 0:rows, :] = moved.reshape(count, rows, 128)

        if level == LEVELS:
            for at in range(cot_chunks):
                cot_copies[at].wait()
                flat = cot[at * chunk : (at + 1) * chunk].reshape(chunk * rows, 256)
                store_parts(select_dot(flat, part_last[...]), at * chunk, chunk)
        else:
            flat = grads[level][:, 0:rows, :].reshape(2 * nx * rows, 128)
            store_parts(select_dot(flat, parts[level - 1]), 0, 2 * nx)

        for s in (1, 0, 2):
            weights = [pattern[level - 1, s * 36 + at] for at in range(36)]

            def step(i):
                for tile in range(tiles):
                    here = tile_rows(tile)
                    there = pl.ds(8 + 8 * tile, 8)
                    values = [
                        turned[w, r, 2 * i + p, here, :]
                        for w in range(3)
                        for p in range(2)
                        for r in range(2)
                    ]
                    totals = [None if s == 1 else tap[t, i + s, there, :] for t in range(3)]
                    for at in range(12):
                        for t in range(3):
                            term = weights[12 * t + at] * values[at]
                            totals[t] = term if totals[t] is None else totals[t] + term
                    for t in range(3):
                        tap[t, i + s, there, :] = totals[t]

            loop(nx, step, UNROLL_MAIN[level])

        target = grads[level - 1]
        first = 1 if level == LEVELS else 0

        def combine(x):
            total = None
            for t in range(3):
                for q in range(2):
                    value = tap[t, x, pl.ds(8 - 2 * t + q, ny + 2, stride=2), :]
                    total = value if total is None else total + value
            keep = inside(level - 1, x, (ny + 2, 128), first, first)
            target[x + first, first : first + ny + 2, :] = jnp.where(keep, total, 0.0)

        loop(nx + 2, combine, UNROLL_SIDE[level])

    def mix_level(level, source, target, weights_of, masked):
        nx, _ = plan.pairs[level]
        weights = [weights_of[level - 1, at] for at in range(16)]
        halves = source.shape[2] // 128

        def step(i):
            for tile in range(plan.rows[level] // 8):
                for half in range(halves):
                    here, lanes = tile_rows(tile), pl.ds(128 * half, 128)
                    mixed = mix(
                        source[2 * i, here, lanes], source[2 * i + 1, here, lanes], weights
                    )
                    for p in range(2):
                        value = mixed[p]
                        if masked:
                            value = value + target[2 * i + p, here, lanes]
                            keep = inside(level, 2 * i + p, (8, 128), 8 * tile, 0)
                            value = jnp.where(keep, value, 0.0)
                        target[2 * i + p, here, lanes] = value

        loop(nx, step, UNROLL_MIX[level])

    adjoint(LEVELS)
    for level in range(LEVELS - 1, 0, -1):
        mix_level(level, grads[level], part[level], mixing_t, False)
        adjoint(level)

    pack(part, send_b, outer, 1)

    @pl.when(jnp.logical_not(first_row))
    def _():
        start_all(out_b)

    mix_level(LEVELS, cot, grad4, mixing_t, False)
    excite_copy.wait()
    mix_level(LEVELS, excite, density, mixing, False)

    @pl.when(first_row)
    def _():
        pl.semaphore_wait(barrier, partners)
        start_all(out_a)
        start_all(out_b)

    wait_received(out_a)
    unpack(recv_a, ext, outer, False)
    for x in range(ext0.shape[0]):
        keep = inside(0, x, ext0.shape[1:], 0, 0)
        ext0[x] = jnp.where(keep, ext0[x], 0.0)

    def forward(level):
        nx, ny = plan.pairs[level]
        rows = plan.rows[level]
        size = plan.block[level][2] // 2
        first = 1 if level == LEVELS else 0
        source = field[level - 1]
        count = up8(ny + 2)

        def widen(x):
            for tile in range(count // 8):
                value = source[x + first, pl.ds(first + 8 * tile, 8), :]
                for w, moved in enumerate((shift_down(value, size), value, shift_up(value, size))):
                    for q in range(2):
                        spread[w, x, pl.ds(16 * tile + q, 8, stride=2), :] = moved

        loop(nx + 2, widen, UNROLL_SIDE[level])

        for s in range(3):
            weights = [pattern[level - 1, s * 36 + at] for at in range(36)]

            def step(i):
                for tile in range(rows // 8):
                    here = tile_rows(tile)
                    totals = [None] * 4
                    for tap in range(9):
                        value = spread[tap % 3, i + s, pl.ds(8 * tile + 2 * (tap // 3), 8), :]
                        for at in range(4):
                            term = weights[tap * 4 + at] * value
                            totals[at] = term if totals[at] is None else totals[at] + term
                    for at in range(4):
                        p, r = at // 2, at % 2
                        value = totals[at]
                        if s:
                            value = value + sums[r, 2 * i + p, here, :]
                        sums[r, 2 * i + p, here, :] = value

            loop(nx, step, UNROLL_MAIN[level])

        def merged(x0, count_x, matrix):
            both = jnp.concatenate(
                [sums[r, x0 : x0 + count_x, 0:rows, :].reshape(count_x * rows, 128) for r in range(2)],
                axis=1,
            )
            return select_dot(both, matrix).reshape(count_x, rows, -1)

        if level < LEVELS:
            field[level][:, 0:rows, :] = merged(0, 2 * nx, merges[level - 1])
            mix_level(level, ext[level], field[level], mixing, True)
        else:
            for at in range(cot_chunks):
                here = slice(at * chunk, (at + 1) * chunk)
                density[here] = density[here] + merged(at * chunk, chunk, merge_last[...])

    for level in range(1, LEVELS + 1):
        forward(level)

    wait_received(out_b)
    unpack(recv_b, part, inner, True)
    for level, target in enumerate((grad0, grad1, grad2, grad3)):
        bx, by, size = plan.block[level]
        target[...] = part[level][2 : 2 + bx, 2 : 2 + by, 0:size]
    wait_sent(out_a)
    wait_sent(out_b)


def finish_kernel(*refs):
    count = (len(refs) - 1) // 2
    copies = [
        pltpu.make_async_copy(refs[at], refs[count + at], refs[-1].at[at]) for at in range(count)
    ]
    for copy in copies:
        copy.start()
    for copy in copies:
        copy.wait()


def pin(array):
    return pltpu.with_memory_space_constraint(array, pltpu.HBM)


def body(
    noise_level0,
    noise_level1,
    noise_level2,
    noise_level3,
    noise_level4,
    refine_kernels,
    noise_kernels,
    cotangent,
):
    noises = (noise_level0, noise_level1, noise_level2, noise_level3, noise_level4)
    plan = Plan([noise.shape for noise in noises])
    nx, ny = plan.pairs[LEVELS]
    rows = plan.rows[LEVELS]
    hbm = pl.BlockSpec(memory_space=pltpu.HBM)
    vmem = pl.BlockSpec(memory_space=pltpu.VMEM)
    size_z = noise_level4.shape[2]

    def scratch(*shape, dtype=F32):
        return pltpu.VMEM(shape, dtype)

    def field_shape(level):
        grown = plan.ext[level]
        return (grown[0], grown[1] + 8, 128)

    count = len(DIRS)
    dma = pltpu.SemaphoreType.DMA
    results = [
        jax.ShapeDtypeStruct(array.shape, F32)
        for array in (noise_level4, *noises[:LEVELS], cotangent)
    ]
    blocks = pl.pallas_call(
        lambda *refs: main_kernel(plan, *refs),
        out_shape=results,
        in_specs=[hbm] * 8,
        out_specs=[vmem] * 6,
        scratch_shapes=[scratch(*noise.shape) for noise in noises[:LEVELS]]
        + [pltpu.SMEM(table.shape, F32) for table in (refine_kernels, noise_kernels)]
        + [scratch(*shape) for shape in plan.ext]
        + [scratch(*shape) for shape in plan.ext]
        + [scratch(*field_shape(level)) for level in (1, 2, 3)]
        + [scratch(*plan.ext[level]) for level in (1, 2, 3)]
        + [
            scratch(3, plan.pairs[level][0] + 2, plan.rows[level] + 16, 128)
            for level in (1, 2, 3, 4)
        ]
        + [
            scratch(LEVELS, 108, 8, 128),
            scratch(LEVELS, 16, 8, 128),
            scratch(LEVELS, 16, 8, 128),
            scratch(LEVELS - 1, 256, 128, dtype=BF16),
            scratch(LEVELS - 1, 128, 256, dtype=BF16),
            scratch(256, size_z, dtype=BF16),
            scratch(size_z, 256, dtype=BF16),
            scratch(*cotangent.shape),
            scratch(*noise_level4.shape),
            scratch(3, nx + 2, 2 * up8(ny + 2), 128),
            scratch(2, 2 * nx, rows, 128),
            scratch(3, 2, 2 * nx, rows, 128),
        ]
        + [scratch(plan.message_rows, 128)] * 4
        + [dma((LEVELS,)), dma((2,)), dma((4,)), dma((1,))]
        + [dma((count,))] * 4,
        compiler_params=pltpu.CompilerParams(
            collective_id=0, has_side_effects=True, vmem_limit_bytes=32 * 1024 * 1024
        ),
    )(*[pin(noise) for noise in noises], pin(refine_kernels), pin(noise_kernels), pin(cotangent))

    return pl.pallas_call(
        finish_kernel,
        out_shape=[pltpu.HBM(result.shape, F32) for result in results],
        in_specs=[vmem] * 6,
        out_specs=[hbm] * 6,
        scratch_shapes=[dma((6,))],
        compiler_params=pltpu.CompilerParams(vmem_limit_bytes=8 * 1024 * 1024),
    )(*blocks)


def solution(mesh):
    placed = P("group", "brick", None)
    return jax.shard_map(
        body,
        mesh=mesh,
        in_specs=(placed,) * 5 + (P(), P(), placed),
        out_specs=(placed,) * 6,
        check_vma=False,
    )
```

```python
import jax
import jax.numpy as jnp
from jax import lax
from jax.experimental import pallas as pl
from jax.experimental.pallas import tpu as pltpu
from jax.sharding import PartitionSpec as P

LEVELS = 4
F32 = jnp.float32
BF16 = jnp.bfloat16
MESH = pl.DeviceIdType.MESH

NEAR = [(dx, dy) for dx in (-1, 0, 1) for dy in (-1, 0, 1) if (dx, dy) != (0, 0)]
FAR = [(dx, dy) for dx in (-2, 2) for dy in (-1, 0, 1)]
DIRS = sorted(NEAR + FAR, key=lambda step: (-step[1], abs(step[0])))


def up8(n):
    return -(-n // 8) * 8


class Plan:
    def __init__(self, shapes):
        self.block = shapes
        self.pairs = {}
        for level in range(1, LEVELS + 1):
            grow = 0 if level == LEVELS else 2
            self.pairs[level] = (shapes[level][0] // 2 + grow, shapes[level][1] // 2 + grow)
        self.rows = {level: up8(2 * ny) for level, (_, ny) in self.pairs.items()}
        self.ext = [
            (shapes[level][0] + 4, up8(shapes[level][1] + 4), 128) for level in range(LEVELS)
        ]
        self.pieces = {}
        self.offset = {}
        total = 0
        for dx, dy in DIRS:
            rows = 0
            pieces = []
            for level in range(LEVELS):
                if abs(dx) == 2 and level > 0:
                    continue
                bx, by = shapes[level][0], shapes[level][1]
                count_x = bx if dx == 0 else min(2, bx)
                count_y = by if dy == 0 else 2
                pieces.append((level, rows, count_x, count_y))
                rows += count_x * count_y
            self.pieces[dx, dy] = pieces
            self.offset[dx, dy] = (total, up8(rows))
            total += up8(rows)
        self.message_rows = total


def inner(step, size):
    if step == 0 or size == 1:
        return 2
    return 2 if step < 0 else size


def outer(step, size):
    if step == 0:
        return 2
    if size == 1:
        return 2 + step
    return 0 if step < 0 else size + 2


def lane_iota(shape):
    return lax.broadcasted_iota(jnp.int32, shape, len(shape) - 1)


def row_iota(shape):
    return lax.broadcasted_iota(jnp.int32, shape, len(shape) - 2)


def split(values):
    high = values.astype(BF16)
    return high, (values - high.astype(F32)).astype(BF16)


def select_dot(values, matrix):
    high, low = split(values)
    return jnp.dot(high, matrix, preferred_element_type=F32) + jnp.dot(
        low, matrix, preferred_element_type=F32
    )


def merge_matrix(size, width):
    row, col = row_iota((256, width)), lane_iota((256, width))
    parity = (row >= 128).astype(jnp.int32)
    at = row - 128 * parity
    return jnp.where((col == 2 * at + parity) & (at < size), 1.0, 0.0).astype(BF16)


def part_matrix(size, width):
    row, col = row_iota((width, 256)), lane_iota((width, 256))
    parity = (col >= 128).astype(jnp.int32)
    at = col - 128 * parity
    return jnp.where((row == 2 * at + parity) & (at < size), 1.0, 0.0).astype(BF16)


def parities():
    shape = (8, 128)
    return row_iota(shape) % 2 == 0, lane_iota(shape) % 2 == 0


def noise_patterns(read, store, transpose):
    even_row, even_lane = parities()
    for p in range(2):
        for other in range(2):
            for dq in range(2):
                for dr in range(2):
                    value = {}
                    for q in range(2):
                        for r in range(2):
                            here = 4 * p + 2 * q + r
                            there = 4 * other + 2 * (q ^ dq) + (r ^ dr)
                            value[q, r] = read(there, here) if transpose else read(here, there)
                    store(
                        p * 8 + other * 4 + dq * 2 + dr,
                        jnp.where(
                            even_row,
                            jnp.where(even_lane, value[0, 0], value[0, 1]),
                            jnp.where(even_lane, value[1, 0], value[1, 1]),
                        ),
                    )


def swaps(tile):
    even_row, even_lane = parities()

    def lanes(v):
        return jnp.where(even_lane, pltpu.roll(v, 127, 1), pltpu.roll(v, 1, 1))

    turned = jnp.where(even_row, pltpu.roll(tile, 7, 0), pltpu.roll(tile, 1, 0))
    return [tile, lanes(tile), turned, lanes(turned)]


def mix(first, second, weights):
    terms = swaps(first) + swaps(second)
    results = []
    for p in range(2):
        total = weights[p * 8] * terms[0]
        for at in range(1, 8):
            total = total + weights[p * 8 + at] * terms[at]
        results.append(total)
    return results


def shift_down(values, size):
    lane = lane_iota(values.shape)
    return jnp.where((lane > 0) & (lane < size), pltpu.roll(values, 1, 1), 0.0)


def shift_up(values, size):
    lane = lane_iota(values.shape)
    return jnp.where(lane < size - 1, pltpu.roll(values, 127, 1), 0.0)


def loop(count, step, unroll):
    if unroll >= count:
        for i in range(count):
            step(i)
        return

    def one(i, carry):
        step(i)
        return carry

    lax.fori_loop(0, count, one, 0, unroll=unroll)


UNROLL_MAIN = {1: 8, 2: 8, 3: 8, 4: 4}
UNROLL_SIDE = {1: 16, 2: 16, 3: 16, 4: 16}
UNROLL_MIX = {1: 16, 2: 16, 3: 16, 4: 2}
LINE = 8


def main_kernel(
    plan,
    noise0, noise1, noise2, noise3, noise4, refine_hbm, noise_hbm, cotangent,
    density, grad0, grad1, grad2, grad3, grad4,
    own0, own1, own2, own3, refine_k, noise_k,
    ext0, ext1, ext2, ext3, part0, part1, part2, part3,
    field1, field2, field3, grads1, grads2, grads3,
    taps1, taps2, taps3, taps4,
    pattern, mixing, mixing_t, wide, merges, parts, merge_last, part_last,
    cot, excite, spread, sums, turned,
    send_a, recv_a, send_b, recv_b,
    own_sem, table_sem, cot_sem, excite_sem,
    send_a_sem, recv_a_sem, send_b_sem, recv_b_sem,
):
    group, brick = lax.axis_index("group"), lax.axis_index("brick")
    groups, bricks = lax.axis_size("group"), lax.axis_size("brick")
    ext = [ext0, ext1, ext2, ext3]
    part = [part0, part1, part2, part3]
    field = [ext0, field1, field2, field3]
    grads = [part0, grads1, grads2, grads3]
    taps = [None, taps1, taps2, taps3, taps4]

    def neighbour(dx, dy):
        return (
            lax.rem(group + (dx + groups), groups),
            lax.rem(brick + (dy + bricks), bricks),
        )

    own = [own0, own1, own2, own3]
    own_copies = []
    for at, source in enumerate((noise0, noise1, noise2, noise3)):
        own_copies.append(pltpu.make_async_copy(source, own[at], own_sem.at[at]))
    table_copies = [
        pltpu.make_async_copy(refine_hbm, refine_k, table_sem.at[0]),
        pltpu.make_async_copy(noise_hbm, noise_k, table_sem.at[1]),
    ]
    cot_chunks = cot_sem.shape[0]
    chunk = cot.shape[0] // cot_chunks
    cot_copies = [
        pltpu.make_async_copy(
            cotangent.at[pl.ds(at * chunk, chunk)], cot.at[pl.ds(at * chunk, chunk)], cot_sem.at[at]
        )
        for at in range(cot_chunks)
    ]
    excite_copy = pltpu.make_async_copy(noise4, excite, excite_sem.at[0])
    for copy in table_copies + cot_copies + own_copies + [excite_copy]:
        copy.start()

    def exists(dx, dy):
        x, y = group + dx, brick + dy
        return (x >= 0) & (x < groups) & (y >= 0) & (y < bricks)

    recv_a[...] = jnp.zeros(recv_a.shape, F32)
    recv_b[...] = jnp.zeros(recv_b.shape, F32)
    barrier = pltpu.get_barrier_semaphore()
    partners = 0
    for dx, dy in DIRS:
        partners = partners + exists(dx, dy).astype(jnp.int32)

        @pl.when(exists(dx, dy))
        def _():
            pl.semaphore_signal(barrier, inc=1, device_id=neighbour(dx, dy), device_id_type=MESH)

    for level in range(LEVELS):
        ext[level][...] = jnp.zeros(ext[level].shape, F32)
        if level:
            grads[level][...] = jnp.zeros(grads[level].shape, F32)
        part[level][...] = jnp.zeros(part[level].shape, F32)
    send_a[...] = jnp.zeros(send_a.shape, F32)
    def pack(source, target, start_of, sign, steps):
        for dx, dy in steps:
            base, _ = plan.offset[dx, dy]
            for level, row, count_x, count_y in plan.pieces[dx, dy]:
                bx, by, _ = plan.block[level]
                x0, y0 = start_of(sign * dx, bx), start_of(sign * dy, by)
                for i in range(count_x):
                    target[pl.ds(base + row + i * count_y, count_y), :] = source[level][
                        x0 + i, y0 : y0 + count_y, :
                    ]

    def unpack(source, target, start_of, add):
        for dx, dy in DIRS:
            base, _ = plan.offset[dx, dy]
            for level, row, count_x, count_y in plan.pieces[dx, dy]:
                bx, by, _ = plan.block[level]
                x0, y0 = start_of(-dx, bx), start_of(-dy, by)
                for i in range(count_x):
                    value = source[pl.ds(base + row + i * count_y, count_y), :]
                    if add:
                        value = value + target[level][x0 + i, y0 : y0 + count_y, :]
                    target[level][x0 + i, y0 : y0 + count_y, :] = value

    def copies(source, target, send_sem, recv_sem):
        made = []
        for at, (dx, dy) in enumerate(DIRS):
            base, rows = plan.offset[dx, dy]
            made.append(
                pltpu.make_async_remote_copy(
                    src_ref=source.at[pl.ds(base, rows)],
                    dst_ref=target.at[pl.ds(base, rows)],
                    send_sem=send_sem.at[at],
                    recv_sem=recv_sem.at[at],
                    device_id=neighbour(dx, dy),
                    device_id_type=MESH,
                )
            )
        return made

    def start(made, steps):
        for (dx, dy), copy in zip(DIRS, made):
            if (dx, dy) in steps:
                pl.when(exists(dx, dy))(copy.start)

    def wait_sent(made):
        for (dx, dy), copy in zip(DIRS, made):
            pl.when(exists(dx, dy))(copy.wait_send)

    def wait_received(made):
        for (dx, dy), copy in zip(DIRS, made):
            pl.when(exists(-dx, -dy))(copy.wait_recv)

    out_a = copies(send_a, recv_a, send_a_sem, recv_a_sem)
    out_b = copies(send_b, recv_b, send_b_sem, recv_b_sem)
    upward = [step for step in DIRS if step[1] > 0]
    others = [step for step in DIRS if step[1] <= 0]
    first_row = lax.rem(brick, LINE) == 0
    last_row = lax.rem(brick, LINE) == LINE - 1
    middle = jnp.logical_not(first_row | last_row)

    send_b[...] = jnp.zeros(send_b.shape, F32)
    for level in range(1, LEVELS + 1):
        nx, _ = plan.pairs[level]
        rows = plan.rows[level]
        for t in range(3):
            for x in range(nx + 2):
                taps[level][t, x, 0:8, :] = jnp.zeros((8, 128), F32)
                taps[level][t, x, 8 + rows : 16 + rows, :] = jnp.zeros((8, 128), F32)
            for x in (0, nx + 1):
                taps[level][t, x, 8 : 8 + rows, :] = jnp.zeros((rows, 128), F32)
        size = plan.block[level][2] // 2
        if level < LEVELS:
            merges[level - 1] = merge_matrix(size, 128)
            parts[level - 1] = part_matrix(size, 128)
        else:
            merge_last[...] = merge_matrix(size, 256)
            part_last[...] = part_matrix(size, 256)
    def build_refine(level):
        for p in range(2):
            for r in range(2):
                first, second = 4 * p + r, 4 * p + 2 + r
                rows = jnp.where(
                    row_iota((8, 27)) % 2 == 0,
                    refine_k[level, first : first + 1, :],
                    refine_k[level, second : second + 1, :],
                )
                for o in range(27):
                    pattern[level, o * 4 + p * 2 + r] = jnp.broadcast_to(
                        rows[:, o : o + 1], (8, 128)
                    )

    def build_mixing(level):
        table = noise_k[level]
        for v in range(8):
            wide[level, v] = jnp.broadcast_to(table[:, v : v + 1], (8, 128))

        def read(u, v):
            return wide[level, v, u : u + 1, :]

        def store(at, value):
            mixing[level, at] = value

        def store_t(at, value):
            mixing_t[level, at] = value

        noise_patterns(read, store, False)
        noise_patterns(read, store_t, True)

    for copy in table_copies:
        copy.wait()
    build_refine(LEVELS - 1)
    for level in range(LEVELS):
        bx, by, size = plan.block[level]
        own_copies[level].wait()
        ext[level][2 : 2 + bx, 2 : 2 + by, 0:size] = own[level][...]

    pack(ext, send_a, inner, 1, DIRS)

    @pl.when(last_row)
    def _():
        pl.semaphore_wait(barrier, partners)
        start(out_a, upward)

    def inside(level, x_at, shape, first_row, first_x):
        bx, by, _ = plan.block[level]
        y = row_iota(shape) + (brick * by - 2 + first_row)
        x = group * bx - 2 + first_x + x_at
        limit = jnp.where((x >= 0) & (x < groups * bx), bricks * by, 0)
        return (y >= 0) & (y < limit)

    def tile_rows(at):
        return pl.ds(8 * at, 8)

    def adjoint(level):
        nx, ny = plan.pairs[level]
        rows = plan.rows[level]
        size = plan.block[level][2] // 2
        tiles = rows // 8
        tap = taps[level]

        def store_parts(both, x0, count):
            for r in range(2):
                flat = both[:, 128 * r : 128 * (r + 1)]
                for w, moved in enumerate((shift_up(flat, size), flat, shift_down(flat, size))):
                    turned[w, r, x0 : x0 + count, 0:rows, :] = moved.reshape(count, rows, 128)

        if level == LEVELS:
            for at in range(cot_chunks):
                cot_copies[at].wait()
                flat = cot[at * chunk : (at + 1) * chunk].reshape(chunk * rows, 256)
                store_parts(select_dot(flat, part_last[...]), at * chunk, chunk)
        else:
            flat = grads[level][:, 0:rows, :].reshape(2 * nx * rows, 128)
            store_parts(select_dot(flat, parts[level - 1]), 0, 2 * nx)

        for s in (1, 0, 2):
            weights = [pattern[level - 1, s * 36 + at] for at in range(36)]

            def step(i):
                for tile in range(tiles):
                    here = tile_rows(tile)
                    there = pl.ds(8 + 8 * tile, 8)
                    values = [
                        turned[w, r, 2 * i + p, here, :]
                        for w in range(3)
                        for p in range(2)
                        for r in range(2)
                    ]
                    totals = [None if s == 1 else tap[t, i + s, there, :] for t in range(3)]
                    for at in range(12):
                        for t in range(3):
                            term = weights[12 * t + at] * values[at]
                            totals[t] = term if totals[t] is None else totals[t] + term
                    for t in range(3):
                        tap[t, i + s, there, :] = totals[t]

            loop(nx, step, UNROLL_MAIN[level])

        target = grads[level - 1]
        first = 1 if level == LEVELS else 0

        def combine(x):
            total = None
            for t in range(3):
                for q in range(2):
                    value = tap[t, x, pl.ds(8 - 2 * t + q, ny + 2, stride=2), :]
                    total = value if total is None else total + value
            keep = inside(level - 1, x, (ny + 2, 128), first, first)
            target[x + first, first : first + ny + 2, :] = jnp.where(keep, total, 0.0)

        loop(nx + 2, combine, UNROLL_SIDE[level])

    def mix_level(level, source, target, weights_of, masked):
        nx, _ = plan.pairs[level]
        weights = [weights_of[level - 1, at] for at in range(16)]
        halves = source.shape[2] // 128

        def step(i):
            for tile in range(plan.rows[level] // 8):
                for half in range(halves):
                    here, lanes = tile_rows(tile), pl.ds(128 * half, 128)
                    mixed = mix(
                        source[2 * i, here, lanes], source[2 * i + 1, here, lanes], weights
                    )
                    for p in range(2):
                        value = mixed[p]
                        if masked:
                            value = value + target[2 * i + p, here, lanes]
                            keep = inside(level, 2 * i + p, (8, 128), 8 * tile, 0)
                            value = jnp.where(keep, value, 0.0)
                        target[2 * i + p, here, lanes] = value

        loop(nx, step, UNROLL_MIX[level])

    adjoint(LEVELS)

    @pl.when(middle)
    def _():
        pl.semaphore_wait(barrier, partners)
        start(out_a, DIRS)

    for level in range(LEVELS - 1, 0, -1):
        build_mixing(level - 1)
        build_refine(level - 1)
        mix_level(level, grads[level], part[level], mixing_t, False)
        adjoint(level)

    pack(part, send_b, outer, 1, upward)

    @pl.when(last_row)
    def _():
        start(out_b, upward)

    pack(part, send_b, outer, 1, others)

    @pl.when(first_row)
    def _():
        pl.semaphore_wait(barrier, partners)

    @pl.when(middle)
    def _():
        start(out_b, DIRS)

    @pl.when(jnp.logical_not(middle))
    def _():
        start(out_a, others)
        start(out_b, others)

    @pl.when(first_row)
    def _():
        start(out_a, upward)
        start(out_b, upward)

    build_mixing(LEVELS - 1)
    mix_level(LEVELS, cot, grad4, mixing_t, False)
    excite_copy.wait()
    mix_level(LEVELS, excite, density, mixing, False)

    wait_received(out_a)
    unpack(recv_a, ext, outer, False)
    for x in range(ext0.shape[0]):
        keep = inside(0, x, ext0.shape[1:], 0, 0)
        ext0[x] = jnp.where(keep, ext0[x], 0.0)

    def forward(level):
        nx, ny = plan.pairs[level]
        rows = plan.rows[level]
        size = plan.block[level][2] // 2
        first = 1 if level == LEVELS else 0
        source = field[level - 1]
        count = up8(ny + 2)

        def widen(x):
            for tile in range(count // 8):
                value = source[x + first, pl.ds(first + 8 * tile, 8), :]
                for w, moved in enumerate((shift_down(value, size), value, shift_up(value, size))):
                    for q in range(2):
                        spread[w, x, pl.ds(16 * tile + q, 8, stride=2), :] = moved

        loop(nx + 2, widen, UNROLL_SIDE[level])

        for s in range(3):
            weights = [pattern[level - 1, s * 36 + at] for at in range(36)]

            def step(i):
                for tile in range(rows // 8):
                    here = tile_rows(tile)
                    totals = [None] * 4
                    for tap in range(9):
                        value = spread[tap % 3, i + s, pl.ds(8 * tile + 2 * (tap // 3), 8), :]
                        for at in range(4):
                            term = weights[tap * 4 + at] * value
                            totals[at] = term if totals[at] is None else totals[at] + term
                    for at in range(4):
                        p, r = at // 2, at % 2
                        value = totals[at]
                        if s:
                            value = value + sums[r, 2 * i + p, here, :]
                        sums[r, 2 * i + p, here, :] = value

            loop(nx, step, UNROLL_MAIN[level])

        def merged(x0, count_x, matrix):
            both = jnp.concatenate(
                [sums[r, x0 : x0 + count_x, 0:rows, :].reshape(count_x * rows, 128) for r in range(2)],
                axis=1,
            )
            return select_dot(both, matrix).reshape(count_x, rows, -1)

        if level < LEVELS:
            field[level][:, 0:rows, :] = merged(0, 2 * nx, merges[level - 1])
            mix_level(level, ext[level], field[level], mixing, True)
        else:
            for at in range(cot_chunks):
                here = slice(at * chunk, (at + 1) * chunk)
                density[here] = density[here] + merged(at * chunk, chunk, merge_last[...])

    for level in range(1, LEVELS + 1):
        forward(level)

    wait_received(out_b)
    unpack(recv_b, part, inner, True)
    for level, target in enumerate((grad0, grad1, grad2, grad3)):
        bx, by, size = plan.block[level]
        target[...] = part[level][2 : 2 + bx, 2 : 2 + by, 0:size]
    wait_sent(out_a)
    wait_sent(out_b)


def finish_kernel(*refs):
    count = (len(refs) - 1) // 2
    copies = [
        pltpu.make_async_copy(refs[at], refs[count + at], refs[-1].at[at]) for at in range(count)
    ]
    for copy in copies:
        copy.start()
    for copy in copies:
        copy.wait()


def pin(array):
    return pltpu.with_memory_space_constraint(array, pltpu.HBM)


def body(
    noise_level0,
    noise_level1,
    noise_level2,
    noise_level3,
    noise_level4,
    refine_kernels,
    noise_kernels,
    cotangent,
):
    noises = (noise_level0, noise_level1, noise_level2, noise_level3, noise_level4)
    plan = Plan([noise.shape for noise in noises])
    nx, ny = plan.pairs[LEVELS]
    rows = plan.rows[LEVELS]
    hbm = pl.BlockSpec(memory_space=pltpu.HBM)
    vmem = pl.BlockSpec(memory_space=pltpu.VMEM)
    size_z = noise_level4.shape[2]

    def scratch(*shape, dtype=F32):
        return pltpu.VMEM(shape, dtype)

    def field_shape(level):
        grown = plan.ext[level]
        return (grown[0], grown[1] + 8, 128)

    count = len(DIRS)
    dma = pltpu.SemaphoreType.DMA
    results = [
        jax.ShapeDtypeStruct(array.shape, F32)
        for array in (noise_level4, *noises[:LEVELS], cotangent)
    ]
    blocks = pl.pallas_call(
        lambda *refs: main_kernel(plan, *refs),
        out_shape=results,
        in_specs=[hbm] * 8,
        out_specs=[vmem] * 6,
        scratch_shapes=[scratch(*noise.shape) for noise in noises[:LEVELS]]
        + [scratch(*table.shape) for table in (refine_kernels, noise_kernels)]
        + [scratch(*shape) for shape in plan.ext]
        + [scratch(*shape) for shape in plan.ext]
        + [scratch(*field_shape(level)) for level in (1, 2, 3)]
        + [scratch(*plan.ext[level]) for level in (1, 2, 3)]
        + [
            scratch(3, plan.pairs[level][0] + 2, plan.rows[level] + 16, 128)
            for level in (1, 2, 3, 4)
        ]
        + [
            scratch(LEVELS, 108, 8, 128),
            scratch(LEVELS, 16, 8, 128),
            scratch(LEVELS, 16, 8, 128),
            scratch(LEVELS, 8, 8, 128),
            scratch(LEVELS - 1, 256, 128, dtype=BF16),
            scratch(LEVELS - 1, 128, 256, dtype=BF16),
            scratch(256, size_z, dtype=BF16),
            scratch(size_z, 256, dtype=BF16),
            scratch(*cotangent.shape),
            scratch(*noise_level4.shape),
            scratch(3, nx + 2, 2 * up8(ny + 2), 128),
            scratch(2, 2 * nx, rows, 128),
            scratch(3, 2, 2 * nx, rows, 128),
        ]
        + [scratch(plan.message_rows, 128)] * 4
        + [dma((LEVELS,)), dma((2,)), dma((4,)), dma((1,))]
        + [dma((count,))] * 4,
        compiler_params=pltpu.CompilerParams(
            collective_id=0, has_side_effects=True, vmem_limit_bytes=32 * 1024 * 1024
        ),
    )(*[pin(noise) for noise in noises], pin(refine_kernels), pin(noise_kernels), pin(cotangent))

    return pl.pallas_call(
        finish_kernel,
        out_shape=[pltpu.HBM(result.shape, F32) for result in results],
        in_specs=[vmem] * 6,
        out_specs=[hbm] * 6,
        scratch_shapes=[dma((6,))],
        compiler_params=pltpu.CompilerParams(vmem_limit_bytes=8 * 1024 * 1024),
    )(*blocks)


def solution(mesh):
    placed = P("group", "brick", None)
    return jax.shard_map(
        body,
        mesh=mesh,
        in_specs=(placed,) * 5 + (P(), P(), placed),
        out_specs=(placed,) * 6,
        check_vma=False,
    )
```

```python
import jax
import jax.numpy as jnp
from jax import lax
from jax.experimental import pallas as pl
from jax.experimental.pallas import tpu as pltpu
from jax.sharding import PartitionSpec as P

LEVELS = 4
F32 = jnp.float32
BF16 = jnp.bfloat16
MESH = pl.DeviceIdType.MESH

NEAR = [(dx, dy) for dx in (-1, 0, 1) for dy in (-1, 0, 1) if (dx, dy) != (0, 0)]
FAR = [(dx, dy) for dx in (-2, 2) for dy in (-1, 0, 1)]
DIRS = sorted(NEAR + FAR, key=lambda step: (-step[1], abs(step[0])))


def up8(n):
    return -(-n // 8) * 8


class Plan:
    def __init__(self, shapes):
        self.block = shapes
        self.pairs = {}
        for level in range(1, LEVELS + 1):
            grow = 0 if level == LEVELS else 2
            self.pairs[level] = (shapes[level][0] // 2 + grow, shapes[level][1] // 2 + grow)
        self.rows = {level: up8(2 * ny) for level, (_, ny) in self.pairs.items()}
        self.ext = [
            (shapes[level][0] + 4, up8(shapes[level][1] + 4), 128) for level in range(LEVELS)
        ]
        self.pieces = {}
        self.offset = {}
        total = 0
        for dx, dy in DIRS:
            rows = 0
            pieces = []
            for level in range(LEVELS):
                if abs(dx) == 2 and level > 0:
                    continue
                bx, by = shapes[level][0], shapes[level][1]
                count_x = bx if dx == 0 else min(2, bx)
                count_y = by if dy == 0 else 2
                pieces.append((level, rows, count_x, count_y))
                rows += count_x * count_y
            self.pieces[dx, dy] = pieces
            self.offset[dx, dy] = (total, up8(rows))
            total += up8(rows)
        self.message_rows = total


def inner(step, size):
    if step == 0 or size == 1:
        return 2
    return 2 if step < 0 else size


def outer(step, size):
    if step == 0:
        return 2
    if size == 1:
        return 2 + step
    return 0 if step < 0 else size + 2


def lane_iota(shape):
    return lax.broadcasted_iota(jnp.int32, shape, len(shape) - 1)


def row_iota(shape):
    return lax.broadcasted_iota(jnp.int32, shape, len(shape) - 2)


def split(values):
    high = values.astype(BF16)
    return high, (values - high.astype(F32)).astype(BF16)


def select_dot(values, matrix):
    high, low = split(values)
    return jnp.dot(high, matrix, preferred_element_type=F32) + jnp.dot(
        low, matrix, preferred_element_type=F32
    )


def merge_matrix(size, width, half):
    row, col = row_iota((2 * half, width)), lane_iota((2 * half, width))
    parity = (row >= half).astype(jnp.int32)
    at = row - half * parity
    return jnp.where((col == 2 * at + parity) & (at < size), 1.0, 0.0).astype(BF16)


def part_matrix(size, width, half, fold):
    row, col = row_iota((width, 2 * half)), lane_iota((width, 2 * half))
    parity = (col >= half).astype(jnp.int32)
    at = col - half * parity
    fine = 2 * at + parity
    found = row == fine
    if fold:
        found = found | (row == fine + half)
    return jnp.where(found & (at < size), 1.0, 0.0).astype(BF16)


def parities():
    shape = (8, 128)
    return row_iota(shape) % 2 == 0, lane_iota(shape) % 2 == 0


def noise_patterns(read, store, transpose):
    even_row, even_lane = parities()
    for p in range(2):
        for other in range(2):
            for dq in range(2):
                for dr in range(2):
                    value = {}
                    for q in range(2):
                        for r in range(2):
                            here = 4 * p + 2 * q + r
                            there = 4 * other + 2 * (q ^ dq) + (r ^ dr)
                            value[q, r] = read(there, here) if transpose else read(here, there)
                    store(
                        p * 8 + other * 4 + dq * 2 + dr,
                        jnp.where(
                            even_row,
                            jnp.where(even_lane, value[0, 0], value[0, 1]),
                            jnp.where(even_lane, value[1, 0], value[1, 1]),
                        ),
                    )


def swaps(tile):
    even_row, even_lane = parities()

    def lanes(v):
        return jnp.where(even_lane, pltpu.roll(v, 127, 1), pltpu.roll(v, 1, 1))

    turned = jnp.where(even_row, pltpu.roll(tile, 7, 0), pltpu.roll(tile, 1, 0))
    return [tile, lanes(tile), turned, lanes(turned)]


def mix(first, second, weights):
    terms = swaps(first) + swaps(second)
    results = []
    for p in range(2):
        total = weights[p * 8] * terms[0]
        for at in range(1, 8):
            total = total + weights[p * 8 + at] * terms[at]
        results.append(total)
    return results


def shift_down(values, size, half):
    lane = lane_iota(values.shape) % half
    return jnp.where((lane > 0) & (lane < size), pltpu.roll(values, 1, 1), 0.0)


def shift_up(values, size, half):
    lane = lane_iota(values.shape) % half
    return jnp.where(lane < size - 1, pltpu.roll(values, 127, 1), 0.0)


def loop(count, step, unroll):
    if unroll >= count:
        for i in range(count):
            step(i)
        return

    def one(i, carry):
        step(i)
        return carry

    lax.fori_loop(0, count, one, 0, unroll=unroll)


UNROLL_MAIN = {1: 8, 2: 8, 3: 8, 4: 4}
UNROLL_SIDE = {1: 16, 2: 16, 3: 16, 4: 16}
UNROLL_MIX = {1: 16, 2: 16, 3: 16, 4: 2}
LINE = 8
HALF = 64


def main_kernel(
    plan,
    noise0, noise1, noise2, noise3, noise4, refine_hbm, noise_hbm, cotangent,
    density, grad0, grad1, grad2, grad3, grad4,
    own0, own1, own2, own3, refine_k, noise_k,
    ext0, ext1, ext2, ext3, part0, part1, part2, part3,
    field1, field2, field3, grads1, grads2, grads3,
    taps1, taps2, taps3, taps4,
    pattern, mixing, mixing_t, wide, merges, parts, merge_last, part_last,
    cot, excite, spread, sums, turned,
    send_a, recv_a, send_b, recv_b,
    own_sem, table_sem, cot_sem, excite_sem,
    send_a_sem, recv_a_sem, send_b_sem, recv_b_sem,
):
    group, brick = lax.axis_index("group"), lax.axis_index("brick")
    groups, bricks = lax.axis_size("group"), lax.axis_size("brick")
    ext = [ext0, ext1, ext2, ext3]
    part = [part0, part1, part2, part3]
    field = [ext0, field1, field2, field3]
    grads = [part0, grads1, grads2, grads3]
    taps = [None, taps1, taps2, taps3, taps4]

    def neighbour(dx, dy):
        return (
            lax.rem(group + (dx + groups), groups),
            lax.rem(brick + (dy + bricks), bricks),
        )

    own = [own0, own1, own2, own3]
    own_copies = []
    for at, source in enumerate((noise0, noise1, noise2, noise3)):
        own_copies.append(pltpu.make_async_copy(source, own[at], own_sem.at[at]))
    table_copies = [
        pltpu.make_async_copy(refine_hbm, refine_k, table_sem.at[0]),
        pltpu.make_async_copy(noise_hbm, noise_k, table_sem.at[1]),
    ]
    cot_chunks = cot_sem.shape[0]
    chunk = cot.shape[0] // cot_chunks
    cot_copies = [
        pltpu.make_async_copy(
            cotangent.at[pl.ds(at * chunk, chunk)], cot.at[pl.ds(at * chunk, chunk)], cot_sem.at[at]
        )
        for at in range(cot_chunks)
    ]
    excite_copy = pltpu.make_async_copy(noise4, excite, excite_sem.at[0])
    for copy in table_copies + cot_copies + own_copies + [excite_copy]:
        copy.start()

    def exists(dx, dy):
        x, y = group + dx, brick + dy
        return (x >= 0) & (x < groups) & (y >= 0) & (y < bricks)

    recv_a[...] = jnp.zeros(recv_a.shape, F32)
    recv_b[...] = jnp.zeros(recv_b.shape, F32)
    barrier = pltpu.get_barrier_semaphore()
    partners = 0
    for dx, dy in DIRS:
        partners = partners + exists(dx, dy).astype(jnp.int32)

        @pl.when(exists(dx, dy))
        def _():
            pl.semaphore_signal(barrier, inc=1, device_id=neighbour(dx, dy), device_id_type=MESH)

    for level in range(LEVELS):
        ext[level][...] = jnp.zeros(ext[level].shape, F32)
        if level:
            grads[level][...] = jnp.zeros(grads[level].shape, F32)
        part[level][...] = jnp.zeros(part[level].shape, F32)
    send_a[...] = jnp.zeros(send_a.shape, F32)
    def pack(source, target, start_of, sign, steps):
        for dx, dy in steps:
            base, _ = plan.offset[dx, dy]
            for level, row, count_x, count_y in plan.pieces[dx, dy]:
                bx, by, _ = plan.block[level]
                x0, y0 = start_of(sign * dx, bx), start_of(sign * dy, by)
                for i in range(count_x):
                    target[pl.ds(base + row + i * count_y, count_y), :] = source[level][
                        x0 + i, y0 : y0 + count_y, :
                    ]

    def unpack(source, target, start_of, add, steps):
        for dx, dy in steps:
            base, _ = plan.offset[dx, dy]
            for level, row, count_x, count_y in plan.pieces[dx, dy]:
                bx, by, _ = plan.block[level]
                x0, y0 = start_of(-dx, bx), start_of(-dy, by)
                for i in range(count_x):
                    value = source[pl.ds(base + row + i * count_y, count_y), :]
                    if add:
                        value = value + target[level][x0 + i, y0 : y0 + count_y, :]
                    target[level][x0 + i, y0 : y0 + count_y, :] = value

    def copies(source, target, send_sem, recv_sem):
        made = []
        for at, (dx, dy) in enumerate(DIRS):
            base, rows = plan.offset[dx, dy]
            made.append(
                pltpu.make_async_remote_copy(
                    src_ref=source.at[pl.ds(base, rows)],
                    dst_ref=target.at[pl.ds(base, rows)],
                    send_sem=send_sem.at[at],
                    recv_sem=recv_sem.at[at],
                    device_id=neighbour(dx, dy),
                    device_id_type=MESH,
                )
            )
        return made

    def start(made, steps):
        for (dx, dy), copy in zip(DIRS, made):
            if (dx, dy) in steps:
                pl.when(exists(dx, dy))(copy.start)

    def wait_sent(made):
        for (dx, dy), copy in zip(DIRS, made):
            pl.when(exists(dx, dy))(copy.wait_send)

    def wait_received(made, steps):
        for (dx, dy), copy in zip(DIRS, made):
            if (dx, dy) in steps:
                pl.when(exists(-dx, -dy))(copy.wait_recv)

    out_a = copies(send_a, recv_a, send_a_sem, recv_a_sem)
    out_b = copies(send_b, recv_b, send_b_sem, recv_b_sem)
    upward = [step for step in DIRS if step[1] > 0]
    others = [step for step in DIRS if step[1] <= 0]
    first_row = lax.rem(brick, LINE) == 0
    last_row = lax.rem(brick, LINE) == LINE - 1
    middle = jnp.logical_not(first_row | last_row)

    send_b[...] = jnp.zeros(send_b.shape, F32)
    for level in range(1, LEVELS + 1):
        nx, _ = plan.pairs[level]
        rows = plan.rows[level]
        for t in range(3):
            for x in range(nx + 2):
                taps[level][t, x, 0:8, :] = jnp.zeros((8, 128), F32)
                taps[level][t, x, 8 + rows : 16 + rows, :] = jnp.zeros((8, 128), F32)
            for x in (0, nx + 1):
                taps[level][t, x, 8 : 8 + rows, :] = jnp.zeros((rows, 128), F32)
        size = plan.block[level][2] // 2
        if level < LEVELS:
            merges[level - 1] = merge_matrix(size, 128, HALF)
            parts[level - 1] = part_matrix(size, 128, HALF, level < LEVELS - 1)
        else:
            merge_last[...] = merge_matrix(size, 256, 128)
            part_last[...] = part_matrix(size, 256, 128, False)
    def build_refine(level):
        low = lane_iota((8, 128)) < HALF
        for p in range(2):
            rows = [
                jnp.where(
                    row_iota((8, 27)) % 2 == 0,
                    refine_k[level, 4 * p + r : 4 * p + r + 1, :],
                    refine_k[level, 4 * p + 2 + r : 4 * p + 3 + r, :],
                )
                for r in range(2)
            ]
            for o in range(27):
                tiles = [jnp.broadcast_to(rows[r][:, o : o + 1], (8, 128)) for r in range(2)]
                if level == LEVELS - 1:
                    for r in range(2):
                        pattern[level, o * 4 + p * 2 + r] = tiles[r]
                else:
                    pattern[level, o * 2 + p] = jnp.where(low, tiles[0], tiles[1])

    def build_mixing(level):
        table = noise_k[level]
        for v in range(8):
            wide[level, v] = jnp.broadcast_to(table[:, v : v + 1], (8, 128))

        def read(u, v):
            return wide[level, v, u : u + 1, :]

        def store(at, value):
            mixing[level, at] = value

        def store_t(at, value):
            mixing_t[level, at] = value

        noise_patterns(read, store, False)
        noise_patterns(read, store_t, True)

    for copy in table_copies:
        copy.wait()
    build_refine(LEVELS - 1)
    for level in range(LEVELS):
        bx, by, size = plan.block[level]
        own_copies[level].wait()
        ext[level][2 : 2 + bx, 2 : 2 + by, 0:size] = own[level][...]

    pack(ext, send_a, inner, 1, DIRS)

    @pl.when(last_row)
    def _():
        pl.semaphore_wait(barrier, partners)
        start(out_a, upward)

    def inside(level, x_at, shape, first_row, first_x):
        bx, by, _ = plan.block[level]
        y = row_iota(shape) + (brick * by - 2 + first_row)
        x = group * bx - 2 + first_x + x_at
        limit = jnp.where((x >= 0) & (x < groups * bx), bricks * by, 0)
        return (y >= 0) & (y < limit)

    def tile_rows(at):
        return pl.ds(8 * at, 8)

    def adjoint(level):
        nx, ny = plan.pairs[level]
        halves, half = (2, 128) if level == LEVELS else (1, HALF)
        rows = plan.rows[level]
        size = plan.block[level][2] // 2
        tiles = rows // 8
        tap = taps[level]

        def store_parts(both, x0, count):
            for r in range(halves):
                flat = both[:, 128 * r : 128 * (r + 1)]
                for w, moved in enumerate(
                    (shift_up(flat, size, half), flat, shift_down(flat, size, half))
                ):
                    turned[w, r, x0 : x0 + count, 0:rows, :] = moved.reshape(count, rows, 128)

        if level == LEVELS:
            for at in range(cot_chunks):
                cot_copies[at].wait()
                flat = cot[at * chunk : (at + 1) * chunk].reshape(chunk * rows, 256)
                store_parts(select_dot(flat, part_last[...]), at * chunk, chunk)
        else:
            flat = grads[level][:, 0:rows, :].reshape(2 * nx * rows, 128)
            store_parts(select_dot(flat, parts[level - 1]), 0, 2 * nx)

        for s in (1, 0, 2):
            weights = [pattern[level - 1, s * 18 * halves + at] for at in range(18 * halves)]

            def step(i):
                for tile in range(tiles):
                    here = tile_rows(tile)
                    there = pl.ds(8 + 8 * tile, 8)
                    values = [
                        turned[w, r, 2 * i + p, here, :]
                        for w in range(3)
                        for p in range(2)
                        for r in range(halves)
                    ]
                    totals = [None if s == 1 else tap[t, i + s, there, :] for t in range(3)]
                    for at in range(6 * halves):
                        for t in range(3):
                            term = weights[6 * halves * t + at] * values[at]
                            totals[t] = term if totals[t] is None else totals[t] + term
                    for t in range(3):
                        tap[t, i + s, there, :] = totals[t]

            loop(nx, step, UNROLL_MAIN[level])

        target = grads[level - 1]
        first = 1 if level == LEVELS else 0

        def combine(x):
            total = None
            for t in range(3):
                for q in range(2):
                    value = tap[t, x, pl.ds(8 - 2 * t + q, ny + 2, stride=2), :]
                    total = value if total is None else total + value
            keep = inside(level - 1, x, (ny + 2, 128), first, first)
            target[x + first, first : first + ny + 2, :] = jnp.where(keep, total, 0.0)

        loop(nx + 2, combine, UNROLL_SIDE[level])

    def mix_level(level, source, target, weights_of, masked, tiles=None):
        nx, _ = plan.pairs[level]
        weights = [weights_of[level - 1, at] for at in range(16)]
        halves = source.shape[2] // 128

        def step(i):
            for tile in range(plan.rows[level] // 8) if tiles is None else tiles:
                for half in range(halves):
                    here, lanes = tile_rows(tile), pl.ds(128 * half, 128)
                    mixed = mix(
                        source[2 * i, here, lanes], source[2 * i + 1, here, lanes], weights
                    )
                    for p in range(2):
                        value = mixed[p]
                        if masked:
                            value = value + target[2 * i + p, here, lanes]
                            keep = inside(level, 2 * i + p, (8, 128), 8 * tile, 0)
                            value = jnp.where(keep, value, 0.0)
                        target[2 * i + p, here, lanes] = value

        loop(nx, step, UNROLL_MIX[level])

    adjoint(LEVELS)

    @pl.when(middle)
    def _():
        pl.semaphore_wait(barrier, partners)
        start(out_a, DIRS)

    def top_tiles(level):
        by = plan.block[level][1]
        return range((by + 2) // 8, (by + 3) // 8 + 1)

    for level in range(LEVELS - 1, 0, -1):
        build_mixing(level - 1)
        build_refine(level - 1)
        mix_level(level, grads[level], part[level], mixing_t, False, top_tiles(level))
        adjoint(level)

    pack(part, send_b, outer, 1, upward)

    @pl.when(last_row)
    def _():
        start(out_b, upward)

    for level in range(LEVELS - 1, 0, -1):
        done = top_tiles(level)
        rest = [tile for tile in range(plan.rows[level] // 8) if tile not in done]
        if rest:
            mix_level(level, grads[level], part[level], mixing_t, False, rest)
    pack(part, send_b, outer, 1, others)

    @pl.when(first_row)
    def _():
        pl.semaphore_wait(barrier, partners)

    @pl.when(middle)
    def _():
        start(out_b, DIRS)

    @pl.when(jnp.logical_not(middle))
    def _():
        start(out_a, others)
        start(out_b, others)

    @pl.when(first_row)
    def _():
        start(out_a, upward)
        start(out_b, upward)

    build_mixing(LEVELS - 1)
    mix_level(LEVELS, cot, grad4, mixing_t, False)
    excite_copy.wait()
    mix_level(LEVELS, excite, density, mixing, False)

    for steps in (others, upward):
        wait_received(out_a, steps)
        unpack(recv_a, ext, outer, False, steps)
    for x in range(ext0.shape[0]):
        keep = inside(0, x, ext0.shape[1:], 0, 0)
        ext0[x] = jnp.where(keep, ext0[x], 0.0)

    def forward(level):
        nx, ny = plan.pairs[level]
        rows = plan.rows[level]
        size = plan.block[level][2] // 2
        first = 1 if level == LEVELS else 0
        halves, half = (2, 128) if level == LEVELS else (1, HALF)
        source = field[level - 1]
        count = up8(ny + 2)

        def widen(x):
            for tile in range(count // 8):
                value = source[x + first, pl.ds(first + 8 * tile, 8), :]
                if level < LEVELS:
                    value = value + pltpu.roll(value, HALF, 1)
                for w, moved in enumerate(
                    (shift_down(value, size, half), value, shift_up(value, size, half))
                ):
                    for q in range(2):
                        spread[w, x, pl.ds(16 * tile + q, 8, stride=2), :] = moved

        loop(nx + 2, widen, UNROLL_SIDE[level])

        for s in range(3):
            weights = [pattern[level - 1, s * 18 * halves + at] for at in range(18 * halves)]

            def step(i):
                for tile in range(rows // 8):
                    here = tile_rows(tile)
                    totals = [None] * (2 * halves)
                    for tap in range(9):
                        value = spread[tap % 3, i + s, pl.ds(8 * tile + 2 * (tap // 3), 8), :]
                        for at in range(2 * halves):
                            term = weights[tap * 2 * halves + at] * value
                            totals[at] = term if totals[at] is None else totals[at] + term
                    for at in range(2 * halves):
                        p, r = at // halves, at % halves
                        value = totals[at]
                        if s:
                            value = value + sums[r, 2 * i + p, here, :]
                        sums[r, 2 * i + p, here, :] = value

            loop(nx, step, UNROLL_MAIN[level])

        def merged(x0, count_x, matrix):
            both = jnp.concatenate(
                [
                    sums[r, x0 : x0 + count_x, 0:rows, :].reshape(count_x * rows, 128)
                    for r in range(halves)
                ],
                axis=1,
            )
            return select_dot(both, matrix).reshape(count_x, rows, -1)

        if level < LEVELS:
            field[level][:, 0:rows, :] = merged(0, 2 * nx, merges[level - 1])
            mix_level(level, ext[level], field[level], mixing, True)
        else:
            for at in range(cot_chunks):
                here = slice(at * chunk, (at + 1) * chunk)
                density[here] = density[here] + merged(at * chunk, chunk, merge_last[...])

    for level in range(1, LEVELS + 1):
        forward(level)

    for steps in (others, upward):
        wait_received(out_b, steps)
        unpack(recv_b, part, inner, True, steps)
    for level, target in enumerate((grad0, grad1, grad2, grad3)):
        bx, by, size = plan.block[level]
        total = part[level][2 : 2 + bx, 2 : 2 + by, 0:size]
        if level < LEVELS - 1:
            total = total + part[level][2 : 2 + bx, 2 : 2 + by, HALF : HALF + size]
        target[...] = total
    wait_sent(out_a)
    wait_sent(out_b)


def finish_kernel(*refs):
    count = (len(refs) - 1) // 2
    copies = [
        pltpu.make_async_copy(refs[at], refs[count + at], refs[-1].at[at]) for at in range(count)
    ]
    for copy in copies:
        copy.start()
    for copy in copies:
        copy.wait()


def pin(array):
    return pltpu.with_memory_space_constraint(array, pltpu.HBM)


def body(
    noise_level0,
    noise_level1,
    noise_level2,
    noise_level3,
    noise_level4,
    refine_kernels,
    noise_kernels,
    cotangent,
):
    noises = (noise_level0, noise_level1, noise_level2, noise_level3, noise_level4)
    plan = Plan([noise.shape for noise in noises])
    nx, ny = plan.pairs[LEVELS]
    rows = plan.rows[LEVELS]
    hbm = pl.BlockSpec(memory_space=pltpu.HBM)
    vmem = pl.BlockSpec(memory_space=pltpu.VMEM)
    size_z = noise_level4.shape[2]

    def scratch(*shape, dtype=F32):
        return pltpu.VMEM(shape, dtype)

    def field_shape(level):
        grown = plan.ext[level]
        return (grown[0], grown[1] + 8, 128)

    count = len(DIRS)
    dma = pltpu.SemaphoreType.DMA
    results = [
        jax.ShapeDtypeStruct(array.shape, F32)
        for array in (noise_level4, *noises[:LEVELS], cotangent)
    ]
    blocks = pl.pallas_call(
        lambda *refs: main_kernel(plan, *refs),
        out_shape=results,
        in_specs=[hbm] * 8,
        out_specs=[vmem] * 6,
        scratch_shapes=[scratch(*noise.shape) for noise in noises[:LEVELS]]
        + [scratch(*table.shape) for table in (refine_kernels, noise_kernels)]
        + [scratch(*shape) for shape in plan.ext]
        + [scratch(*shape) for shape in plan.ext]
        + [scratch(*field_shape(level)) for level in (1, 2, 3)]
        + [scratch(*plan.ext[level]) for level in (1, 2, 3)]
        + [
            scratch(3, plan.pairs[level][0] + 2, plan.rows[level] + 16, 128)
            for level in (1, 2, 3, 4)
        ]
        + [
            scratch(LEVELS, 108, 8, 128),
            scratch(LEVELS, 16, 8, 128),
            scratch(LEVELS, 16, 8, 128),
            scratch(LEVELS, 8, 8, 128),
            scratch(LEVELS - 1, 128, 128, dtype=BF16),
            scratch(LEVELS - 1, 128, 128, dtype=BF16),
            scratch(256, size_z, dtype=BF16),
            scratch(size_z, 256, dtype=BF16),
            scratch(*cotangent.shape),
            scratch(*noise_level4.shape),
            scratch(3, nx + 2, 2 * up8(ny + 2), 128),
            scratch(2, 2 * nx, rows, 128),
            scratch(3, 2, 2 * nx, rows, 128),
        ]
        + [scratch(plan.message_rows, 128)] * 4
        + [dma((LEVELS,)), dma((2,)), dma((4,)), dma((1,))]
        + [dma((count,))] * 4,
        compiler_params=pltpu.CompilerParams(
            collective_id=0, has_side_effects=True, vmem_limit_bytes=32 * 1024 * 1024
        ),
    )(*[pin(noise) for noise in noises], pin(refine_kernels), pin(noise_kernels), pin(cotangent))

    return pl.pallas_call(
        finish_kernel,
        out_shape=[pltpu.HBM(result.shape, F32) for result in results],
        in_specs=[vmem] * 6,
        out_specs=[hbm] * 6,
        scratch_shapes=[dma((6,))],
        compiler_params=pltpu.CompilerParams(vmem_limit_bytes=8 * 1024 * 1024),
    )(*blocks)


def solution(mesh):
    placed = P("group", "brick", None)
    return jax.shard_map(
        body,
        mesh=mesh,
        in_specs=(placed,) * 5 + (P(), P(), placed),
        out_specs=(placed,) * 6,
        check_vma=False,
    )
```

```python
import jax
import jax.numpy as jnp
from jax import lax
from jax.experimental import pallas as pl
from jax.experimental.pallas import tpu as pltpu
from jax.sharding import PartitionSpec as P

LEVELS = 4
F32 = jnp.float32
BF16 = jnp.bfloat16
MESH = pl.DeviceIdType.MESH

NEAR = [(dx, dy) for dx in (-1, 0, 1) for dy in (-1, 0, 1) if (dx, dy) != (0, 0)]
FAR = [(dx, dy) for dx in (-2, 2) for dy in (-1, 0, 1)]
DIRS = sorted(NEAR + FAR, key=lambda step: (-step[1], abs(step[0])))


def up8(n):
    return -(-n // 8) * 8


class Plan:
    def __init__(self, shapes):
        self.block = shapes
        self.pairs = {}
        for level in range(1, LEVELS + 1):
            grow = 0 if level == LEVELS else 2
            self.pairs[level] = (shapes[level][0] // 2 + grow, shapes[level][1] // 2 + grow)
        self.rows = {level: up8(2 * ny) for level, (_, ny) in self.pairs.items()}
        self.ext = [
            (shapes[level][0] + 4, up8(shapes[level][1] + 4), 128) for level in range(LEVELS)
        ]
        self.pieces = {}
        self.offset = {}
        total = 0
        for dx, dy in DIRS:
            rows = 0
            pieces = []
            for level in range(LEVELS):
                if abs(dx) == 2 and level > 0:
                    continue
                bx, by = shapes[level][0], shapes[level][1]
                count_x = bx if dx == 0 else min(2, bx)
                count_y = by if dy == 0 else 2
                pieces.append((level, rows, count_x, count_y))
                rows += count_x * count_y
            self.pieces[dx, dy] = pieces
            self.offset[dx, dy] = (total, up8(rows))
            total += up8(rows)
        self.message_rows = total


def inner(step, size):
    if step == 0 or size == 1:
        return 2
    return 2 if step < 0 else size


def outer(step, size):
    if step == 0:
        return 2
    if size == 1:
        return 2 + step
    return 0 if step < 0 else size + 2


def lane_iota(shape):
    return lax.broadcasted_iota(jnp.int32, shape, len(shape) - 1)


def row_iota(shape):
    return lax.broadcasted_iota(jnp.int32, shape, len(shape) - 2)


def split(values):
    high = values.astype(BF16)
    return high, (values - high.astype(F32)).astype(BF16)


def select_dot(values, matrix):
    high, low = split(values)
    return jnp.dot(high, matrix, preferred_element_type=F32) + jnp.dot(
        low, matrix, preferred_element_type=F32
    )


def merge_matrix(size, width, half):
    row, col = row_iota((2 * half, width)), lane_iota((2 * half, width))
    parity = (row >= half).astype(jnp.int32)
    at = row - half * parity
    return jnp.where((col == 2 * at + parity) & (at < size), 1.0, 0.0).astype(BF16)


def part_matrix(size, width, half, fold):
    row, col = row_iota((width, 2 * half)), lane_iota((width, 2 * half))
    parity = (col >= half).astype(jnp.int32)
    at = col - half * parity
    fine = 2 * at + parity
    found = row == fine
    if fold:
        found = found | (row == fine + half)
    return jnp.where(found & (at < size), 1.0, 0.0).astype(BF16)


def parities():
    shape = (8, 128)
    return row_iota(shape) % 2 == 0, lane_iota(shape) % 2 == 0


def noise_patterns(read, store, transpose):
    even_row, even_lane = parities()
    for p in range(2):
        for other in range(2):
            for dq in range(2):
                for dr in range(2):
                    value = {}
                    for q in range(2):
                        for r in range(2):
                            here = 4 * p + 2 * q + r
                            there = 4 * other + 2 * (q ^ dq) + (r ^ dr)
                            value[q, r] = read(there, here) if transpose else read(here, there)
                    store(
                        p * 8 + other * 4 + dq * 2 + dr,
                        jnp.where(
                            even_row,
                            jnp.where(even_lane, value[0, 0], value[0, 1]),
                            jnp.where(even_lane, value[1, 0], value[1, 1]),
                        ),
                    )


def swaps(tile):
    even_row, even_lane = parities()

    def lanes(v):
        return jnp.where(even_lane, pltpu.roll(v, 127, 1), pltpu.roll(v, 1, 1))

    turned = jnp.where(even_row, pltpu.roll(tile, 7, 0), pltpu.roll(tile, 1, 0))
    return [tile, lanes(tile), turned, lanes(turned)]


def mix(first, second, weights):
    terms = swaps(first) + swaps(second)
    results = []
    for p in range(2):
        total = weights[p * 8] * terms[0]
        for at in range(1, 8):
            total = total + weights[p * 8 + at] * terms[at]
        results.append(total)
    return results


def shift_down(values, size, half):
    lane = lane_iota(values.shape) % half
    return jnp.where((lane > 0) & (lane < size), pltpu.roll(values, 1, 1), 0.0)


def shift_up(values, size, half):
    lane = lane_iota(values.shape) % half
    return jnp.where(lane < size - 1, pltpu.roll(values, 127, 1), 0.0)


def loop(count, step, unroll):
    if unroll >= count:
        for i in range(count):
            step(i)
        return

    def one(i, carry):
        step(i)
        return carry

    lax.fori_loop(0, count, one, 0, unroll=unroll)


UNROLL_MAIN = {1: 8, 2: 8, 3: 8, 4: 8}
UNROLL_SIDE = {1: 16, 2: 16, 3: 16, 4: 16}
UNROLL_MIX = {1: 16, 2: 16, 3: 16, 4: 4}
LINE = 8
HALF = 64


def main_kernel(
    plan,
    noise0, noise1, noise2, noise3, noise4, refine_hbm, noise_hbm, cotangent,
    density, grad0, grad1, grad2, grad3, grad4,
    own0, own1, own2, own3, refine_k, noise_k,
    ext0, ext1, ext2, ext3, part0, part1, part2, part3,
    field1, field2, field3, grads1, grads2, grads3,
    taps1, taps2, taps3, taps4,
    pattern, mixing, mixing_t, wide, merges, parts, merge_last, part_last,
    cot, excite, spread, sums, turned,
    send_a, recv_a, send_b, recv_b,
    own_sem, table_sem, cot_sem, excite_sem,
    send_a_sem, recv_a_sem, send_b_sem, recv_b_sem,
):
    group, brick = lax.axis_index("group"), lax.axis_index("brick")
    groups, bricks = lax.axis_size("group"), lax.axis_size("brick")
    ext = [ext0, ext1, ext2, ext3]
    part = [part0, part1, part2, part3]
    field = [ext0, field1, field2, field3]
    grads = [part0, grads1, grads2, grads3]
    taps = [None, taps1, taps2, taps3, taps4]

    def neighbour(dx, dy):
        return (
            lax.rem(group + (dx + groups), groups),
            lax.rem(brick + (dy + bricks), bricks),
        )

    own = [own0, own1, own2, own3]
    own_copies = []
    for at, source in enumerate((noise0, noise1, noise2, noise3)):
        own_copies.append(pltpu.make_async_copy(source, own[at], own_sem.at[at]))
    table_copies = [
        pltpu.make_async_copy(refine_hbm, refine_k, table_sem.at[0]),
        pltpu.make_async_copy(noise_hbm, noise_k, table_sem.at[1]),
    ]
    cot_chunks = cot_sem.shape[0]
    chunk = cot.shape[0] // cot_chunks
    cot_copies = [
        pltpu.make_async_copy(
            cotangent.at[pl.ds(at * chunk, chunk)], cot.at[pl.ds(at * chunk, chunk)], cot_sem.at[at]
        )
        for at in range(cot_chunks)
    ]
    excite_copy = pltpu.make_async_copy(noise4, excite, excite_sem.at[0])
    for copy in cot_copies + table_copies + own_copies + [excite_copy]:
        copy.start()

    def exists(dx, dy):
        x, y = group + dx, brick + dy
        return (x >= 0) & (x < groups) & (y >= 0) & (y < bricks)

    recv_a[...] = jnp.zeros(recv_a.shape, F32)
    recv_b[...] = jnp.zeros(recv_b.shape, F32)
    barrier = pltpu.get_barrier_semaphore()
    partners = 0
    for dx, dy in DIRS:
        partners = partners + exists(dx, dy).astype(jnp.int32)

        @pl.when(exists(dx, dy))
        def _():
            pl.semaphore_signal(barrier, inc=1, device_id=neighbour(dx, dy), device_id_type=MESH)

    for level in range(LEVELS):
        ext[level][...] = jnp.zeros(ext[level].shape, F32)
        if level:
            grads[level][...] = jnp.zeros(grads[level].shape, F32)
        part[level][...] = jnp.zeros(part[level].shape, F32)
    send_a[...] = jnp.zeros(send_a.shape, F32)
    def pack(source, target, start_of, sign, steps):
        for dx, dy in steps:
            base, _ = plan.offset[dx, dy]
            for level, row, count_x, count_y in plan.pieces[dx, dy]:
                bx, by, _ = plan.block[level]
                x0, y0 = start_of(sign * dx, bx), start_of(sign * dy, by)
                for i in range(count_x):
                    target[pl.ds(base + row + i * count_y, count_y), :] = source[level][
                        x0 + i, y0 : y0 + count_y, :
                    ]

    def unpack(source, target, start_of, add, steps):
        for dx, dy in steps:
            base, _ = plan.offset[dx, dy]
            for level, row, count_x, count_y in plan.pieces[dx, dy]:
                bx, by, _ = plan.block[level]
                x0, y0 = start_of(-dx, bx), start_of(-dy, by)
                for i in range(count_x):
                    value = source[pl.ds(base + row + i * count_y, count_y), :]
                    if add:
                        value = value + target[level][x0 + i, y0 : y0 + count_y, :]
                    target[level][x0 + i, y0 : y0 + count_y, :] = value

    def copies(source, target, send_sem, recv_sem):
        made = []
        for at, (dx, dy) in enumerate(DIRS):
            base, rows = plan.offset[dx, dy]
            made.append(
                pltpu.make_async_remote_copy(
                    src_ref=source.at[pl.ds(base, rows)],
                    dst_ref=target.at[pl.ds(base, rows)],
                    send_sem=send_sem.at[at],
                    recv_sem=recv_sem.at[at],
                    device_id=neighbour(dx, dy),
                    device_id_type=MESH,
                )
            )
        return made

    def start(made, steps):
        for (dx, dy), copy in zip(DIRS, made):
            if (dx, dy) in steps:
                pl.when(exists(dx, dy))(copy.start)

    def wait_sent(made):
        for (dx, dy), copy in zip(DIRS, made):
            pl.when(exists(dx, dy))(copy.wait_send)

    def wait_received(made, steps):
        for (dx, dy), copy in zip(DIRS, made):
            if (dx, dy) in steps:
                pl.when(exists(-dx, -dy))(copy.wait_recv)

    out_a = copies(send_a, recv_a, send_a_sem, recv_a_sem)
    out_b = copies(send_b, recv_b, send_b_sem, recv_b_sem)
    upward = [step for step in DIRS if step[1] > 0]
    others = [step for step in DIRS if step[1] <= 0]
    first_row = lax.rem(brick, LINE) == 0
    last_row = lax.rem(brick, LINE) == LINE - 1
    middle = jnp.logical_not(first_row | last_row)

    send_b[...] = jnp.zeros(send_b.shape, F32)
    for level in range(1, LEVELS + 1):
        nx, _ = plan.pairs[level]
        rows = plan.rows[level]
        for t in range(3):
            for x in range(nx + 2):
                taps[level][t, x, 0:8, :] = jnp.zeros((8, 128), F32)
                taps[level][t, x, 8 + rows : 16 + rows, :] = jnp.zeros((8, 128), F32)
            for x in (0, nx + 1):
                taps[level][t, x, 8 : 8 + rows, :] = jnp.zeros((rows, 128), F32)
        size = plan.block[level][2] // 2
        if level < LEVELS:
            merges[level - 1] = merge_matrix(size, 128, HALF)
            parts[level - 1] = part_matrix(size, 128, HALF, level < LEVELS - 1)
        else:
            merge_last[...] = merge_matrix(size, 256, 128)
            part_last[...] = part_matrix(size, 256, 128, False)
    def build_refine(level):
        low = lane_iota((8, 128)) < HALF
        for p in range(2):
            rows = [
                jnp.where(
                    row_iota((8, 27)) % 2 == 0,
                    refine_k[level, 4 * p + r : 4 * p + r + 1, :],
                    refine_k[level, 4 * p + 2 + r : 4 * p + 3 + r, :],
                )
                for r in range(2)
            ]
            for o in range(27):
                tiles = [jnp.broadcast_to(rows[r][:, o : o + 1], (8, 128)) for r in range(2)]
                if level == LEVELS - 1:
                    for r in range(2):
                        pattern[level, o * 4 + p * 2 + r] = tiles[r]
                else:
                    pattern[level, o * 2 + p] = jnp.where(low, tiles[0], tiles[1])

    def build_mixing(level):
        table = noise_k[level]
        for v in range(8):
            wide[level, v] = jnp.broadcast_to(table[:, v : v + 1], (8, 128))

        def read(u, v):
            return wide[level, v, u : u + 1, :]

        def store(at, value):
            mixing[level, at] = value

        def store_t(at, value):
            mixing_t[level, at] = value

        noise_patterns(read, store, False)
        noise_patterns(read, store_t, True)

    for copy in table_copies:
        copy.wait()
    build_refine(LEVELS - 1)
    for level in range(LEVELS):
        bx, by, size = plan.block[level]
        own_copies[level].wait()
        ext[level][2 : 2 + bx, 2 : 2 + by, 0:size] = own[level][...]

    pack(ext, send_a, inner, 1, DIRS)

    @pl.when(last_row)
    def _():
        pl.semaphore_wait(barrier, partners)
        start(out_a, upward)

    def inside(level, x_at, shape, first_row, first_x):
        bx, by, _ = plan.block[level]
        y = row_iota(shape) + (brick * by - 2 + first_row)
        x = group * bx - 2 + first_x + x_at
        limit = jnp.where((x >= 0) & (x < groups * bx), bricks * by, 0)
        return (y >= 0) & (y < limit)

    def tile_rows(at):
        return pl.ds(8 * at, 8)

    def adjoint(level):
        nx, ny = plan.pairs[level]
        halves, half = (2, 128) if level == LEVELS else (1, HALF)
        rows = plan.rows[level]
        size = plan.block[level][2] // 2
        tiles = rows // 8
        tap = taps[level]

        def store_parts(both, x0, count):
            for r in range(halves):
                flat = both[:, 128 * r : 128 * (r + 1)]
                for w, moved in enumerate(
                    (shift_up(flat, size, half), flat, shift_down(flat, size, half))
                ):
                    turned[w, r, x0 : x0 + count, 0:rows, :] = moved.reshape(count, rows, 128)

        if level == LEVELS:
            for at in range(cot_chunks):
                cot_copies[at].wait()
                flat = cot[at * chunk : (at + 1) * chunk].reshape(chunk * rows, 256)
                store_parts(select_dot(flat, part_last[...]), at * chunk, chunk)
        else:
            flat = grads[level][:, 0:rows, :].reshape(2 * nx * rows, 128)
            store_parts(select_dot(flat, parts[level - 1]), 0, 2 * nx)

        for s in (1, 0, 2):
            weights = [pattern[level - 1, s * 18 * halves + at] for at in range(18 * halves)]

            def step(i):
                for tile in range(tiles):
                    here = tile_rows(tile)
                    there = pl.ds(8 + 8 * tile, 8)
                    values = [
                        turned[w, r, 2 * i + p, here, :]
                        for w in range(3)
                        for p in range(2)
                        for r in range(halves)
                    ]
                    totals = [None if s == 1 else tap[t, i + s, there, :] for t in range(3)]
                    for at in range(6 * halves):
                        for t in range(3):
                            term = weights[6 * halves * t + at] * values[at]
                            totals[t] = term if totals[t] is None else totals[t] + term
                    for t in range(3):
                        tap[t, i + s, there, :] = totals[t]

            loop(nx, step, UNROLL_MAIN[level])

        target = grads[level - 1]
        first = 1 if level == LEVELS else 0

        def combine(x):
            total = None
            for t in range(3):
                for q in range(2):
                    value = tap[t, x, pl.ds(8 - 2 * t + q, ny + 2, stride=2), :]
                    total = value if total is None else total + value
            keep = inside(level - 1, x, (ny + 2, 128), first, first)
            target[x + first, first : first + ny + 2, :] = jnp.where(keep, total, 0.0)

        loop(nx + 2, combine, UNROLL_SIDE[level])

    def mix_level(level, source, target, weights_of, masked, tiles=None):
        nx, _ = plan.pairs[level]
        weights = [weights_of[level - 1, at] for at in range(16)]
        halves = source.shape[2] // 128

        def step(i):
            for tile in range(plan.rows[level] // 8) if tiles is None else tiles:
                for half in range(halves):
                    here, lanes = tile_rows(tile), pl.ds(128 * half, 128)
                    mixed = mix(
                        source[2 * i, here, lanes], source[2 * i + 1, here, lanes], weights
                    )
                    for p in range(2):
                        value = mixed[p]
                        if masked:
                            value = value + target[2 * i + p, here, lanes]
                            keep = inside(level, 2 * i + p, (8, 128), 8 * tile, 0)
                            value = jnp.where(keep, value, 0.0)
                        target[2 * i + p, here, lanes] = value

        loop(nx, step, UNROLL_MIX[level])

    adjoint(LEVELS)

    @pl.when(middle)
    def _():
        pl.semaphore_wait(barrier, partners)
        start(out_a, DIRS)

    def top_tiles(level):
        by = plan.block[level][1]
        return range((by + 2) // 8, (by + 3) // 8 + 1)

    for level in range(LEVELS - 1, 0, -1):
        build_mixing(level - 1)
        build_refine(level - 1)
        mix_level(level, grads[level], part[level], mixing_t, False, top_tiles(level))
        adjoint(level)

    pack(part, send_b, outer, 1, upward)

    @pl.when(last_row)
    def _():
        start(out_b, upward)

    for level in range(LEVELS - 1, 0, -1):
        done = top_tiles(level)
        rest = [tile for tile in range(plan.rows[level] // 8) if tile not in done]
        if rest:
            mix_level(level, grads[level], part[level], mixing_t, False, rest)
    pack(part, send_b, outer, 1, others)

    @pl.when(first_row)
    def _():
        pl.semaphore_wait(barrier, partners)

    @pl.when(middle)
    def _():
        start(out_b, DIRS)

    @pl.when(jnp.logical_not(middle))
    def _():
        start(out_a, others)
        start(out_b, others)

    @pl.when(first_row)
    def _():
        start(out_a, upward)
        start(out_b, upward)

    build_mixing(LEVELS - 1)
    mix_level(LEVELS, cot, grad4, mixing_t, False)
    excite_copy.wait()
    mix_level(LEVELS, excite, density, mixing, False)

    for steps in (others, upward):
        wait_received(out_a, steps)
        unpack(recv_a, ext, outer, False, steps)
    for x in range(ext0.shape[0]):
        keep = inside(0, x, ext0.shape[1:], 0, 0)
        ext0[x] = jnp.where(keep, ext0[x], 0.0)

    def forward(level):
        nx, ny = plan.pairs[level]
        rows = plan.rows[level]
        size = plan.block[level][2] // 2
        first = 1 if level == LEVELS else 0
        halves, half = (2, 128) if level == LEVELS else (1, HALF)
        source = field[level - 1]
        count = up8(ny + 2)

        def widen(x):
            for tile in range(count // 8):
                value = source[x + first, pl.ds(first + 8 * tile, 8), :]
                if level < LEVELS:
                    value = value + pltpu.roll(value, HALF, 1)
                for w, moved in enumerate(
                    (shift_down(value, size, half), value, shift_up(value, size, half))
                ):
                    for q in range(2):
                        spread[w, x, pl.ds(16 * tile + q, 8, stride=2), :] = moved

        loop(nx + 2, widen, UNROLL_SIDE[level])

        for s in range(3):
            weights = [pattern[level - 1, s * 18 * halves + at] for at in range(18 * halves)]

            def step(i):
                for tile in range(rows // 8):
                    here = tile_rows(tile)
                    totals = [None] * (2 * halves)
                    for tap in range(9):
                        value = spread[tap % 3, i + s, pl.ds(8 * tile + 2 * (tap // 3), 8), :]
                        for at in range(2 * halves):
                            term = weights[tap * 2 * halves + at] * value
                            totals[at] = term if totals[at] is None else totals[at] + term
                    for at in range(2 * halves):
                        p, r = at // halves, at % halves
                        value = totals[at]
                        if s:
                            value = value + sums[r, 2 * i + p, here, :]
                        sums[r, 2 * i + p, here, :] = value

            loop(nx, step, UNROLL_MAIN[level])

        def merged(x0, count_x, matrix):
            both = jnp.concatenate(
                [
                    sums[r, x0 : x0 + count_x, 0:rows, :].reshape(count_x * rows, 128)
                    for r in range(halves)
                ],
                axis=1,
            )
            return select_dot(both, matrix).reshape(count_x, rows, -1)

        if level < LEVELS:
            field[level][:, 0:rows, :] = merged(0, 2 * nx, merges[level - 1])
            mix_level(level, ext[level], field[level], mixing, True)
        else:
            for at in range(cot_chunks):
                here = slice(at * chunk, (at + 1) * chunk)
                density[here] = density[here] + merged(at * chunk, chunk, merge_last[...])

    for level in range(1, LEVELS + 1):
        forward(level)

    wait_sent(out_a)
    for steps in (others, upward):
        if steps is upward:
            wait_sent(out_b)
        wait_received(out_b, steps)
        unpack(recv_b, part, inner, True, steps)
    for level, target in enumerate((grad0, grad1, grad2, grad3)):
        bx, by, size = plan.block[level]
        total = part[level][2 : 2 + bx, 2 : 2 + by, 0:size]
        if level < LEVELS - 1:
            total = total + part[level][2 : 2 + bx, 2 : 2 + by, HALF : HALF + size]
        target[...] = total


def finish_kernel(*refs):
    count = (len(refs) - 1) // 2
    copies = [
        pltpu.make_async_copy(refs[at], refs[count + at], refs[-1].at[at]) for at in range(count)
    ]
    for copy in copies:
        copy.start()
    for copy in copies:
        copy.wait()


def pin(array):
    return pltpu.with_memory_space_constraint(array, pltpu.HBM)


def body(
    noise_level0,
    noise_level1,
    noise_level2,
    noise_level3,
    noise_level4,
    refine_kernels,
    noise_kernels,
    cotangent,
):
    noises = (noise_level0, noise_level1, noise_level2, noise_level3, noise_level4)
    plan = Plan([noise.shape for noise in noises])
    nx, ny = plan.pairs[LEVELS]
    rows = plan.rows[LEVELS]
    hbm = pl.BlockSpec(memory_space=pltpu.HBM)
    vmem = pl.BlockSpec(memory_space=pltpu.VMEM)
    size_z = noise_level4.shape[2]

    def scratch(*shape, dtype=F32):
        return pltpu.VMEM(shape, dtype)

    def field_shape(level):
        grown = plan.ext[level]
        return (grown[0], grown[1] + 8, 128)

    count = len(DIRS)
    dma = pltpu.SemaphoreType.DMA
    results = [
        jax.ShapeDtypeStruct(array.shape, F32)
        for array in (noise_level4, *noises[:LEVELS], cotangent)
    ]
    blocks = pl.pallas_call(
        lambda *refs: main_kernel(plan, *refs),
        out_shape=results,
        in_specs=[hbm] * 8,
        out_specs=[vmem] * 6,
        scratch_shapes=[scratch(*noise.shape) for noise in noises[:LEVELS]]
        + [scratch(*table.shape) for table in (refine_kernels, noise_kernels)]
        + [scratch(*shape) for shape in plan.ext]
        + [scratch(*shape) for shape in plan.ext]
        + [scratch(*field_shape(level)) for level in (1, 2, 3)]
        + [scratch(*plan.ext[level]) for level in (1, 2, 3)]
        + [
            scratch(3, plan.pairs[level][0] + 2, plan.rows[level] + 16, 128)
            for level in (1, 2, 3, 4)
        ]
        + [
            scratch(LEVELS, 108, 8, 128),
            scratch(LEVELS, 16, 8, 128),
            scratch(LEVELS, 16, 8, 128),
            scratch(LEVELS, 8, 8, 128),
            scratch(LEVELS - 1, 128, 128, dtype=BF16),
            scratch(LEVELS - 1, 128, 128, dtype=BF16),
            scratch(256, size_z, dtype=BF16),
            scratch(size_z, 256, dtype=BF16),
            scratch(*cotangent.shape),
            scratch(*noise_level4.shape),
            scratch(3, nx + 2, 2 * up8(ny + 2), 128),
            scratch(2, 2 * nx, rows, 128),
            scratch(3, 2, 2 * nx, rows, 128),
        ]
        + [scratch(plan.message_rows, 128)] * 4
        + [dma((LEVELS,)), dma((2,)), dma((1,)), dma((1,))]
        + [dma((count,))] * 4,
        compiler_params=pltpu.CompilerParams(
            collective_id=0, has_side_effects=True, vmem_limit_bytes=32 * 1024 * 1024
        ),
    )(*[pin(noise) for noise in noises], pin(refine_kernels), pin(noise_kernels), pin(cotangent))

    return pl.pallas_call(
        finish_kernel,
        out_shape=[pltpu.HBM(result.shape, F32) for result in results],
        in_specs=[vmem] * 6,
        out_specs=[hbm] * 6,
        scratch_shapes=[dma((6,))],
        compiler_params=pltpu.CompilerParams(vmem_limit_bytes=8 * 1024 * 1024),
    )(*blocks)


def solution(mesh):
    placed = P("group", "brick", None)
    return jax.shard_map(
        body,
        mesh=mesh,
        in_specs=(placed,) * 5 + (P(), P(), placed),
        out_specs=(placed,) * 6,
        check_vma=False,
    )
```

```python
import jax
import jax.numpy as jnp
from jax import lax
from jax.experimental import pallas as pl
from jax.experimental.pallas import tpu as pltpu
from jax.sharding import PartitionSpec as P

LEVELS = 4
F32 = jnp.float32
BF16 = jnp.bfloat16
MESH = pl.DeviceIdType.MESH

NEAR = [(dx, dy) for dx in (-1, 0, 1) for dy in (-1, 0, 1) if (dx, dy) != (0, 0)]
FAR = [(dx, dy) for dx in (-2, 2) for dy in (-1, 0, 1)]
DIRS = sorted(NEAR + FAR, key=lambda step: (-step[1], abs(step[0])))


def up8(n):
    return -(-n // 8) * 8


class Plan:
    def __init__(self, shapes):
        self.block = shapes
        self.pairs = {}
        for level in range(1, LEVELS + 1):
            grow = 0 if level == LEVELS else 2
            self.pairs[level] = (shapes[level][0] // 2 + grow, shapes[level][1] // 2 + grow)
        self.rows = {level: up8(2 * ny) for level, (_, ny) in self.pairs.items()}
        self.ext = [
            (shapes[level][0] + 4, up8(shapes[level][1] + 4), 128) for level in range(LEVELS)
        ]
        self.pieces = {}
        self.offset = {}
        total = 0
        for dx, dy in DIRS:
            rows = 0
            pieces = []
            for level in range(LEVELS):
                if abs(dx) == 2 and level > 0:
                    continue
                bx, by = shapes[level][0], shapes[level][1]
                count_x = bx if dx == 0 else min(2, bx)
                count_y = by if dy == 0 else 2
                pieces.append((level, rows, count_x, count_y))
                rows += count_x * count_y
            self.pieces[dx, dy] = pieces
            self.offset[dx, dy] = (total, up8(rows))
            total += up8(rows)
        self.message_rows = total


def inner(step, size):
    if step == 0 or size == 1:
        return 2
    return 2 if step < 0 else size


def outer(step, size):
    if step == 0:
        return 2
    if size == 1:
        return 2 + step
    return 0 if step < 0 else size + 2


def lane_iota(shape):
    return lax.broadcasted_iota(jnp.int32, shape, len(shape) - 1)


def row_iota(shape):
    return lax.broadcasted_iota(jnp.int32, shape, len(shape) - 2)


def split(values):
    high = values.astype(BF16)
    return high, (values - high.astype(F32)).astype(BF16)


def select_dot(values, matrix):
    high, low = split(values)
    return jnp.dot(high, matrix, preferred_element_type=F32) + jnp.dot(
        low, matrix, preferred_element_type=F32
    )


def merge_matrix(size, width, half):
    row, col = row_iota((2 * half, width)), lane_iota((2 * half, width))
    parity = (row >= half).astype(jnp.int32)
    at = row - half * parity
    return jnp.where((col == 2 * at + parity) & (at < size), 1.0, 0.0).astype(BF16)


def part_matrix(size, width, half, fold):
    row, col = row_iota((width, 2 * half)), lane_iota((width, 2 * half))
    parity = (col >= half).astype(jnp.int32)
    at = col - half * parity
    fine = 2 * at + parity
    found = row == fine
    if fold:
        found = found | (row == fine + half)
    return jnp.where(found & (at < size), 1.0, 0.0).astype(BF16)


def parities():
    shape = (8, 128)
    return row_iota(shape) % 2 == 0, lane_iota(shape) % 2 == 0


def noise_patterns(read, store, transpose):
    even_row, even_lane = parities()
    for p in range(2):
        for other in range(2):
            for dq in range(2):
                for dr in range(2):
                    value = {}
                    for q in range(2):
                        for r in range(2):
                            here = 4 * p + 2 * q + r
                            there = 4 * other + 2 * (q ^ dq) + (r ^ dr)
                            value[q, r] = read(there, here) if transpose else read(here, there)
                    store(
                        p * 8 + other * 4 + dq * 2 + dr,
                        jnp.where(
                            even_row,
                            jnp.where(even_lane, value[0, 0], value[0, 1]),
                            jnp.where(even_lane, value[1, 0], value[1, 1]),
                        ),
                    )


def swaps(tile):
    even_row, even_lane = parities()

    def lanes(v):
        return jnp.where(even_lane, pltpu.roll(v, 127, 1), pltpu.roll(v, 1, 1))

    turned = jnp.where(even_row, pltpu.roll(tile, 7, 0), pltpu.roll(tile, 1, 0))
    return [tile, lanes(tile), turned, lanes(turned)]


def mix(first, second, weights):
    terms = swaps(first) + swaps(second)
    results = []
    for p in range(2):
        total = weights[p * 8] * terms[0]
        for at in range(1, 8):
            total = total + weights[p * 8 + at] * terms[at]
        results.append(total)
    return results


def shift_down(values, size, half):
    lane = lane_iota(values.shape) % half
    return jnp.where((lane > 0) & (lane < size), pltpu.roll(values, 1, 1), 0.0)


def shift_up(values, size, half):
    lane = lane_iota(values.shape) % half
    return jnp.where(lane < size - 1, pltpu.roll(values, 127, 1), 0.0)


def loop(count, step, unroll):
    if unroll >= count:
        for i in range(count):
            step(i)
        return

    def one(i, carry):
        step(i)
        return carry

    lax.fori_loop(0, count, one, 0, unroll=unroll)


UNROLL_MAIN = {1: 8, 2: 8, 3: 8, 4: 8}
UNROLL_SIDE = {1: 16, 2: 16, 3: 16, 4: 16}
UNROLL_MIX = {1: 16, 2: 16, 3: 16, 4: 4}
LINE = 8
HALF = 64


def main_kernel(
    plan,
    noise0, noise1, noise2, noise3, noise4, refine_hbm, noise_hbm, cotangent,
    density, grad0, grad1, grad2, grad3, grad4,
    own0, own1, own2, own3, refine_k, noise_k,
    ext0, ext1, ext2, ext3, part0, part1, part2, part3,
    field1, field2, field3, grads1, grads2, grads3,
    taps1, taps2, taps3, taps4,
    pattern, mixing, mixing_t, wide, merges, parts, merge_last, part_last,
    cot, excite, spread, sums, turned,
    send_a, recv_a, send_b, recv_b,
    own_sem, table_sem, cot_sem, excite_sem,
    send_a_sem, recv_a_sem, send_b_sem, recv_b_sem,
):
    group, brick = lax.axis_index("group"), lax.axis_index("brick")
    groups, bricks = lax.axis_size("group"), lax.axis_size("brick")
    ext = [ext0, ext1, ext2, ext3]
    part = [part0, part1, part2, part3]
    field = [ext0, field1, field2, field3]
    grads = [part0, grads1, grads2, grads3]
    taps = [None, taps1, taps2, taps3, taps4]

    def neighbour(dx, dy):
        return (
            lax.rem(group + (dx + groups), groups),
            lax.rem(brick + (dy + bricks), bricks),
        )

    own = [own0, own1, own2, own3]
    own_copies = []
    for at, source in enumerate((noise0, noise1, noise2, noise3)):
        own_copies.append(pltpu.make_async_copy(source, own[at], own_sem.at[at]))
    table_copies = [
        pltpu.make_async_copy(refine_hbm, refine_k, table_sem.at[0]),
        pltpu.make_async_copy(noise_hbm, noise_k, table_sem.at[1]),
    ]
    cot_chunks = cot_sem.shape[0]
    chunk = cot.shape[0] // cot_chunks
    cot_copies = [
        pltpu.make_async_copy(
            cotangent.at[pl.ds(at * chunk, chunk)], cot.at[pl.ds(at * chunk, chunk)], cot_sem.at[at]
        )
        for at in range(cot_chunks)
    ]
    excite_copy = pltpu.make_async_copy(noise4, excite, excite_sem.at[0])
    for copy in cot_copies + table_copies + own_copies + [excite_copy]:
        copy.start()

    def exists(dx, dy):
        x, y = group + dx, brick + dy
        return (x >= 0) & (x < groups) & (y >= 0) & (y < bricks)

    recv_a[...] = jnp.zeros(recv_a.shape, F32)
    recv_b[...] = jnp.zeros(recv_b.shape, F32)
    barrier = pltpu.get_barrier_semaphore()
    partners = 0
    for dx, dy in DIRS:
        partners = partners + exists(dx, dy).astype(jnp.int32)

        @pl.when(exists(dx, dy))
        def _():
            pl.semaphore_signal(barrier, inc=1, device_id=neighbour(dx, dy), device_id_type=MESH)

    for level in range(LEVELS):
        ext[level][...] = jnp.zeros(ext[level].shape, F32)
        if level:
            grads[level][...] = jnp.zeros(grads[level].shape, F32)
        part[level][...] = jnp.zeros(part[level].shape, F32)
    send_a[...] = jnp.zeros(send_a.shape, F32)
    def pack(source, target, start_of, sign, steps):
        for dx, dy in steps:
            base, _ = plan.offset[dx, dy]
            for level, row, count_x, count_y in plan.pieces[dx, dy]:
                bx, by, _ = plan.block[level]
                x0, y0 = start_of(sign * dx, bx), start_of(sign * dy, by)
                for i in range(count_x):
                    target[pl.ds(base + row + i * count_y, count_y), :] = source[level][
                        x0 + i, y0 : y0 + count_y, :
                    ]

    def unpack(source, target, start_of, add, steps):
        for dx, dy in steps:
            base, _ = plan.offset[dx, dy]
            for level, row, count_x, count_y in plan.pieces[dx, dy]:
                bx, by, _ = plan.block[level]
                x0, y0 = start_of(-dx, bx), start_of(-dy, by)
                for i in range(count_x):
                    value = source[pl.ds(base + row + i * count_y, count_y), :]
                    if add:
                        value = value + target[level][x0 + i, y0 : y0 + count_y, :]
                    target[level][x0 + i, y0 : y0 + count_y, :] = value

    def copies(source, target, send_sem, recv_sem):
        made = []
        for at, (dx, dy) in enumerate(DIRS):
            base, rows = plan.offset[dx, dy]
            made.append(
                pltpu.make_async_remote_copy(
                    src_ref=source.at[pl.ds(base, rows)],
                    dst_ref=target.at[pl.ds(base, rows)],
                    send_sem=send_sem.at[at],
                    recv_sem=recv_sem.at[at],
                    device_id=neighbour(dx, dy),
                    device_id_type=MESH,
                )
            )
        return made

    def start(made, steps):
        for (dx, dy), copy in zip(DIRS, made):
            if (dx, dy) in steps:
                pl.when(exists(dx, dy))(copy.start)

    def wait_sent(made):
        for (dx, dy), copy in zip(DIRS, made):
            pl.when(exists(dx, dy))(copy.wait_send)

    def wait_received(made, steps):
        for (dx, dy), copy in zip(DIRS, made):
            if (dx, dy) in steps:
                pl.when(exists(-dx, -dy))(copy.wait_recv)

    out_a = copies(send_a, recv_a, send_a_sem, recv_a_sem)
    out_b = copies(send_b, recv_b, send_b_sem, recv_b_sem)
    upward = [step for step in DIRS if step[1] > 0]
    others = [step for step in DIRS if step[1] <= 0]
    first_row = lax.rem(brick, LINE) == 0
    last_row = lax.rem(brick, LINE) == LINE - 1
    middle = jnp.logical_not(first_row | last_row)

    send_b[...] = jnp.zeros(send_b.shape, F32)
    for level in range(1, LEVELS + 1):
        nx, _ = plan.pairs[level]
        rows = plan.rows[level]
        for t in range(3):
            for x in range(nx + 2):
                taps[level][t, x, 0:8, :] = jnp.zeros((8, 128), F32)
                taps[level][t, x, 8 + rows : 16 + rows, :] = jnp.zeros((8, 128), F32)
            for x in (0, nx + 1):
                taps[level][t, x, 8 : 8 + rows, :] = jnp.zeros((rows, 128), F32)
        size = plan.block[level][2] // 2
        if level < LEVELS:
            merges[level - 1] = merge_matrix(size, 128, HALF)
            parts[level - 1] = part_matrix(size, 128, HALF, level < LEVELS - 1)
        else:
            merge_last[...] = merge_matrix(size, 256, 128)
            part_last[...] = part_matrix(size, 256, 128, False)
    def build_refine(level):
        low = lane_iota((8, 128)) < HALF
        for p in range(2):
            rows = [
                jnp.where(
                    row_iota((8, 27)) % 2 == 0,
                    refine_k[level, 4 * p + r : 4 * p + r + 1, :],
                    refine_k[level, 4 * p + 2 + r : 4 * p + 3 + r, :],
                )
                for r in range(2)
            ]
            for o in range(27):
                tiles = [jnp.broadcast_to(rows[r][:, o : o + 1], (8, 128)) for r in range(2)]
                if level == LEVELS - 1:
                    for r in range(2):
                        pattern[level, o * 4 + p * 2 + r] = tiles[r]
                else:
                    pattern[level, o * 2 + p] = jnp.where(low, tiles[0], tiles[1])

    def spread_mixing(level):
        table = noise_k[level]
        for v in range(8):
            wide[level, v] = jnp.broadcast_to(table[:, v : v + 1], (8, 128))

    def build_mixing(level, target, transpose):
        def read(u, v):
            return wide[level, v, u : u + 1, :]

        def store(at, value):
            target[level, at] = value

        noise_patterns(read, store, transpose)

    for copy in table_copies:
        copy.wait()
    build_refine(LEVELS - 1)
    for level in range(LEVELS):
        bx, by, size = plan.block[level]
        own_copies[level].wait()
        ext[level][2 : 2 + bx, 2 : 2 + by, 0:size] = own[level][...]

    pack(ext, send_a, inner, 1, DIRS)

    @pl.when(last_row)
    def _():
        pl.semaphore_wait(barrier, partners)
        start(out_a, upward)

    def inside(level, x_at, shape, first_row, first_x):
        bx, by, _ = plan.block[level]
        y = row_iota(shape) + (brick * by - 2 + first_row)
        x = group * bx - 2 + first_x + x_at
        limit = jnp.where((x >= 0) & (x < groups * bx), bricks * by, 0)
        return (y >= 0) & (y < limit)

    def tile_rows(at):
        return pl.ds(8 * at, 8)

    def adjoint(level):
        nx, ny = plan.pairs[level]
        halves, half = (2, 128) if level == LEVELS else (1, HALF)
        rows = plan.rows[level]
        size = plan.block[level][2] // 2
        tiles = rows // 8
        tap = taps[level]

        def store_parts(both, x0, count):
            for r in range(halves):
                flat = both[:, 128 * r : 128 * (r + 1)]
                for w, moved in enumerate(
                    (shift_up(flat, size, half), flat, shift_down(flat, size, half))
                ):
                    turned[w, r, x0 : x0 + count, 0:rows, :] = moved.reshape(count, rows, 128)

        if level == LEVELS:
            for at in range(cot_chunks):
                cot_copies[at].wait()
                flat = cot[at * chunk : (at + 1) * chunk].reshape(chunk * rows, 256)
                store_parts(select_dot(flat, part_last[...]), at * chunk, chunk)
        else:
            flat = grads[level][:, 0:rows, :].reshape(2 * nx * rows, 128)
            store_parts(select_dot(flat, parts[level - 1]), 0, 2 * nx)

        for s in (1, 0, 2):
            weights = [pattern[level - 1, s * 18 * halves + at] for at in range(18 * halves)]

            def step(i):
                for tile in range(tiles):
                    here = tile_rows(tile)
                    there = pl.ds(8 + 8 * tile, 8)
                    values = [
                        turned[w, r, 2 * i + p, here, :]
                        for w in range(3)
                        for p in range(2)
                        for r in range(halves)
                    ]
                    totals = [None if s == 1 else tap[t, i + s, there, :] for t in range(3)]
                    for at in range(6 * halves):
                        for t in range(3):
                            term = weights[6 * halves * t + at] * values[at]
                            totals[t] = term if totals[t] is None else totals[t] + term
                    for t in range(3):
                        tap[t, i + s, there, :] = totals[t]

            loop(nx, step, UNROLL_MAIN[level])

        target = grads[level - 1]
        first = 1 if level == LEVELS else 0

        def combine(x):
            total = None
            for t in range(3):
                for q in range(2):
                    value = tap[t, x, pl.ds(8 - 2 * t + q, ny + 2, stride=2), :]
                    total = value if total is None else total + value
            keep = inside(level - 1, x, (ny + 2, 128), first, first)
            target[x + first, first : first + ny + 2, :] = jnp.where(keep, total, 0.0)

        loop(nx + 2, combine, UNROLL_SIDE[level])

    def mix_level(level, source, target, weights_of, masked, tiles=None):
        nx, _ = plan.pairs[level]
        weights = [weights_of[level - 1, at] for at in range(16)]
        halves = source.shape[2] // 128

        def step(i):
            for tile in range(plan.rows[level] // 8) if tiles is None else tiles:
                for half in range(halves):
                    here, lanes = tile_rows(tile), pl.ds(128 * half, 128)
                    mixed = mix(
                        source[2 * i, here, lanes], source[2 * i + 1, here, lanes], weights
                    )
                    for p in range(2):
                        value = mixed[p]
                        if masked:
                            value = value + target[2 * i + p, here, lanes]
                            keep = inside(level, 2 * i + p, (8, 128), 8 * tile, 0)
                            value = jnp.where(keep, value, 0.0)
                        target[2 * i + p, here, lanes] = value

        loop(nx, step, UNROLL_MIX[level])

    adjoint(LEVELS)

    @pl.when(middle)
    def _():
        pl.semaphore_wait(barrier, partners)
        start(out_a, DIRS)

    def top_tiles(level):
        by = plan.block[level][1]
        return range((by + 2) // 8, (by + 3) // 8 + 1)

    for level in range(LEVELS - 1, 0, -1):
        spread_mixing(level - 1)
        build_mixing(level - 1, mixing_t, True)
        build_refine(level - 1)
        mix_level(level, grads[level], part[level], mixing_t, False, top_tiles(level))
        adjoint(level)

    pack(part, send_b, outer, 1, upward)

    @pl.when(last_row)
    def _():
        start(out_b, upward)

    for level in range(LEVELS - 1, 0, -1):
        done = top_tiles(level)
        rest = [tile for tile in range(plan.rows[level] // 8) if tile not in done]
        if rest:
            mix_level(level, grads[level], part[level], mixing_t, False, rest)
    pack(part, send_b, outer, 1, others)

    @pl.when(first_row)
    def _():
        pl.semaphore_wait(barrier, partners)

    @pl.when(middle)
    def _():
        start(out_b, DIRS)

    @pl.when(jnp.logical_not(middle))
    def _():
        start(out_a, others)
        start(out_b, others)

    @pl.when(first_row)
    def _():
        start(out_a, upward)
        start(out_b, upward)

    spread_mixing(LEVELS - 1)
    build_mixing(LEVELS - 1, mixing_t, True)
    for level in range(LEVELS):
        build_mixing(level, mixing, False)
    mix_level(LEVELS, cot, grad4, mixing_t, False)
    excite_copy.wait()
    mix_level(LEVELS, excite, density, mixing, False)

    for steps in (others, upward):
        wait_received(out_a, steps)
        unpack(recv_a, ext, outer, False, steps)
    for x in range(ext0.shape[0]):
        keep = inside(0, x, ext0.shape[1:], 0, 0)
        ext0[x] = jnp.where(keep, ext0[x], 0.0)

    def forward(level):
        nx, ny = plan.pairs[level]
        rows = plan.rows[level]
        size = plan.block[level][2] // 2
        first = 1 if level == LEVELS else 0
        halves, half = (2, 128) if level == LEVELS else (1, HALF)
        source = field[level - 1]
        count = up8(ny + 2)

        def widen(x):
            for tile in range(count // 8):
                value = source[x + first, pl.ds(first + 8 * tile, 8), :]
                if level < LEVELS:
                    value = value + pltpu.roll(value, HALF, 1)
                for w, moved in enumerate(
                    (shift_down(value, size, half), value, shift_up(value, size, half))
                ):
                    for q in range(2):
                        spread[w, x, pl.ds(16 * tile + q, 8, stride=2), :] = moved

        loop(nx + 2, widen, UNROLL_SIDE[level])

        for s in range(3):
            weights = [pattern[level - 1, s * 18 * halves + at] for at in range(18 * halves)]

            def step(i):
                for tile in range(rows // 8):
                    here = tile_rows(tile)
                    totals = [None] * (2 * halves)
                    for tap in range(9):
                        value = spread[tap % 3, i + s, pl.ds(8 * tile + 2 * (tap // 3), 8), :]
                        for at in range(2 * halves):
                            term = weights[tap * 2 * halves + at] * value
                            totals[at] = term if totals[at] is None else totals[at] + term
                    for at in range(2 * halves):
                        p, r = at // halves, at % halves
                        value = totals[at]
                        if s:
                            value = value + sums[r, 2 * i + p, here, :]
                        sums[r, 2 * i + p, here, :] = value

            loop(nx, step, UNROLL_MAIN[level])

        def merged(x0, count_x, matrix):
            both = jnp.concatenate(
                [
                    sums[r, x0 : x0 + count_x, 0:rows, :].reshape(count_x * rows, 128)
                    for r in range(halves)
                ],
                axis=1,
            )
            return select_dot(both, matrix).reshape(count_x, rows, -1)

        if level < LEVELS:
            field[level][:, 0:rows, :] = merged(0, 2 * nx, merges[level - 1])
            mix_level(level, ext[level], field[level], mixing, True)
        else:
            for at in range(cot_chunks):
                here = slice(at * chunk, (at + 1) * chunk)
                density[here] = density[here] + merged(at * chunk, chunk, merge_last[...])

    for level in range(1, LEVELS + 1):
        forward(level)

    wait_sent(out_a)
    for steps in (others, upward):
        if steps is upward:
            wait_sent(out_b)
        wait_received(out_b, steps)
        unpack(recv_b, part, inner, True, steps)
    for level, target in enumerate((grad0, grad1, grad2, grad3)):
        bx, by, size = plan.block[level]
        total = part[level][2 : 2 + bx, 2 : 2 + by, 0:size]
        if level < LEVELS - 1:
            total = total + part[level][2 : 2 + bx, 2 : 2 + by, HALF : HALF + size]
        target[...] = total


def finish_kernel(*refs):
    count = (len(refs) - 1) // 2
    copies = [
        pltpu.make_async_copy(refs[at], refs[count + at], refs[-1].at[at]) for at in range(count)
    ]
    for copy in copies:
        copy.start()
    for copy in copies:
        copy.wait()


def pin(array):
    return pltpu.with_memory_space_constraint(array, pltpu.HBM)


def body(
    noise_level0,
    noise_level1,
    noise_level2,
    noise_level3,
    noise_level4,
    refine_kernels,
    noise_kernels,
    cotangent,
):
    noises = (noise_level0, noise_level1, noise_level2, noise_level3, noise_level4)
    plan = Plan([noise.shape for noise in noises])
    nx, ny = plan.pairs[LEVELS]
    rows = plan.rows[LEVELS]
    hbm = pl.BlockSpec(memory_space=pltpu.HBM)
    vmem = pl.BlockSpec(memory_space=pltpu.VMEM)
    size_z = noise_level4.shape[2]

    def scratch(*shape, dtype=F32):
        return pltpu.VMEM(shape, dtype)

    def field_shape(level):
        grown = plan.ext[level]
        return (grown[0], grown[1] + 8, 128)

    count = len(DIRS)
    dma = pltpu.SemaphoreType.DMA
    results = [
        jax.ShapeDtypeStruct(array.shape, F32)
        for array in (noise_level4, *noises[:LEVELS], cotangent)
    ]
    blocks = pl.pallas_call(
        lambda *refs: main_kernel(plan, *refs),
        out_shape=results,
        in_specs=[hbm] * 8,
        out_specs=[vmem] * 6,
        scratch_shapes=[scratch(*noise.shape) for noise in noises[:LEVELS]]
        + [scratch(*table.shape) for table in (refine_kernels, noise_kernels)]
        + [scratch(*shape) for shape in plan.ext]
        + [scratch(*shape) for shape in plan.ext]
        + [scratch(*field_shape(level)) for level in (1, 2, 3)]
        + [scratch(*plan.ext[level]) for level in (1, 2, 3)]
        + [
            scratch(3, plan.pairs[level][0] + 2, plan.rows[level] + 16, 128)
            for level in (1, 2, 3, 4)
        ]
        + [
            scratch(LEVELS, 108, 8, 128),
            scratch(LEVELS, 16, 8, 128),
            scratch(LEVELS, 16, 8, 128),
            scratch(LEVELS, 8, 8, 128),
            scratch(LEVELS - 1, 128, 128, dtype=BF16),
            scratch(LEVELS - 1, 128, 128, dtype=BF16),
            scratch(256, size_z, dtype=BF16),
            scratch(size_z, 256, dtype=BF16),
            scratch(*cotangent.shape),
            scratch(*noise_level4.shape),
            scratch(3, nx + 2, 2 * up8(ny + 2) + 8, 128),
            scratch(2, 2 * nx, rows, 128),
            scratch(3, 2, 2 * nx, rows, 128),
        ]
        + [scratch(plan.message_rows, 128)] * 4
        + [dma((LEVELS,)), dma((2,)), dma((1,)), dma((1,))]
        + [dma((count,))] * 4,
        compiler_params=pltpu.CompilerParams(
            collective_id=0, has_side_effects=True, vmem_limit_bytes=32 * 1024 * 1024
        ),
    )(*[pin(noise) for noise in noises], pin(refine_kernels), pin(noise_kernels), pin(cotangent))

    return pl.pallas_call(
        finish_kernel,
        out_shape=[pltpu.HBM(result.shape, F32) for result in results],
        in_specs=[vmem] * 6,
        out_specs=[hbm] * 6,
        scratch_shapes=[dma((6,))],
        compiler_params=pltpu.CompilerParams(vmem_limit_bytes=8 * 1024 * 1024),
    )(*blocks)


def solution(mesh):
    placed = P("group", "brick", None)
    return jax.shard_map(
        body,
        mesh=mesh,
        in_specs=(placed,) * 5 + (P(), P(), placed),
        out_specs=(placed,) * 6,
        check_vma=False,
    )
```
